32 devices in a mesh: dp: 16 (over z, y, x), tensor: 2 (over core).
Axes of the slice: x: 2, y: 2, z: 4, core: 2. Of those that a mesh axis runs over, the one named last changes fastest.
Arguments:
- layer_input: bfloat16 [8192, 1536], P('dp'), may hold values from -6 to 6
- doc_lengths: int32 [16, 4], P('dp'), may hold values from 0 to 512, as said below
- routes: int32 [8192, 8], P('dp'), may hold values from 0 to 15, all different within a row; in each aligned block of 512 rows (0 to 511, 512 to 1023, ...) at most 288 rows name the same one
- norm1_gain: bfloat16 [1536], replicated, may hold values from 0.5 to 1.5
- w_query: bfloat16 [1536, 1536], P(None, 'tensor'), may hold values from -0.15625 to 0.15625
- w_key: bfloat16 [1536, 512], P(None, 'tensor'), may hold values from -0.15625 to 0.15625
- w_value: bfloat16 [1536, 512], P(None, 'tensor'), may hold values from -0.15625 to 0.15625
- w_out: bfloat16 [1536, 1536], P('tensor'), may hold values from -0.625 to 0.625
- norm2_gain: bfloat16 [1536], replicated, may hold values from 0.5 to 1.5
- w_router: bfloat16 [1536, 16], replicated, may hold values from -0.078125 to 0.078125
- w_gate: bfloat16 [16, 1536, 512], P('dp', None, 'tensor'), may hold values from -0.15625 to 0.15625
- w_up: bfloat16 [16, 1536, 512], P('dp', None, 'tensor'), may hold values from -0.15625 to 0.15625
- w_down: bfloat16 [16, 512, 1536], P('dp', 'tensor'), may hold values from -0.75 to 0.75
- cotangent: bfloat16 [8192, 1536], P('dp'), may hold values from -6 to 6
Outputs:
- layer_output: bfloat16 [8192, 1536], P('dp')
- grad_x: bfloat16 [8192, 1536], P('dp')
- grad_norm1: float32 [1536], replicated
- grad_query: float32 [1536, 1536], P(None, 'tensor')
- grad_key: float32 [1536, 512], P(None, 'tensor')
- grad_value: float32 [1536, 512], P(None, 'tensor')
- grad_out: float32 [1536, 1536], P('tensor')
- grad_norm2: float32 [1536], replicated
- grad_router: float32 [1536, 16], replicated
- grad_gate: float32 [16, 1536, 512], P('dp', None, 'tensor')
- grad_up: float32 [16, 1536, 512], P('dp', None, 'tensor')
- grad_down: float32 [16, 512, 1536], P('dp', 'tensor')
The draws below stay inside these ranges and needn't reach their ends.
Inputs may be any that keep to these rules, and one draw needn't show every extreme that they name: `doc_lengths`: each index of dp has 4 lengths summing to 512; a length may be zero; some index holds one sequence of all 512 tokens. `routes`: A token's 8 experts differ. In the 512 rows of one index of dp no expert is named more than 288 times, a bound that some block reaches.
All inputs are finite; a program needn't handle non-finite values.
Results may differ from the reference program's by a relative error of at most 0.02.
Values may be sent and summed in bfloat16 or wider, within the bound.
No kernel may reach another device: no remote copies, remote signals or barrier semaphores. Data moves between devices by JAX's collectives and lax.ppermute only.
A program may use at most 320 MiB of HBM per device.

```python
import math
import jax
import jax.numpy as jnp
import numpy as np
from jax import lax

D = 1536
HEADS = 24
KV_HEADS = 8
HEAD_DIM = 64
FF = 512
TOPK = 8
TOK_DEV = 512
SEQS = 4
EXPERTS = 16
SPLIT = 1
CAP = 288
TOKENS = 8192
N_DP = 16
N_TENSOR = 2


def draw_doc_lengths(key, part):
    cut_points = jax.random.randint(jax.random.fold_in(key, 11), (N_DP, SEQS - 1), 0, TOK_DEV + 1)
    cut_points = jnp.sort(cut_points, axis=1)
    boundaries = jnp.concatenate([jnp.zeros((N_DP, 1), jnp.int32), cut_points.astype(jnp.int32), jnp.full((N_DP, 1), TOK_DEV, jnp.int32)], axis=1)
    lengths = boundaries[:, 1:] - boundaries[:, :-1]
    full_device = jax.random.randint(jax.random.fold_in(key, 12), (), 0, N_DP)
    single = jnp.zeros((SEQS,), jnp.int32).at[0].set(TOK_DEV)
    chosen_row = (jnp.arange(N_DP, dtype=jnp.int32) == full_device)[:, None]
    return jnp.where(chosen_row, single[None, :], lengths).astype(jnp.int32)


def block_levels(stream_key, shape, cuts, smallest, high):
    loudness, own = 1.0, jax.random.fold_in(stream_key, 6)
    for axis_at, parts in cuts:
        steps = jnp.exp(jax.random.uniform(jax.random.fold_in(own, axis_at), (parts,), jnp.float32, smallest / len(cuts), high / len(cuts)))
        loudness = loudness * jnp.repeat(steps, shape[axis_at] // parts).reshape([-1 if axis == axis_at else 1 for axis in range(len(shape))])
    return loudness


def assign_block(own_key, own, number, rows, number_of, top, bound, slope):
    sequence = jax.random.permutation(own_key, number_of)
    packed, common = load_shares(number_of, rows * top, bound, slope, True), load_shares(number_of, rows * top, bound, slope, False)
    places = jnp.arange(number_of)

    def named(sizes, turn):
        used = int((sizes > 0).sum())
        fixed = max(1, used // 4)
        shifted = fixed + (places - fixed + turn * (used - fixed)) % max(1, number_of - fixed)
        return jnp.zeros((number_of,), jnp.int32).at[sequence[jnp.where(places < fixed, places, shifted)]].set(jnp.asarray(sizes, jnp.int32))

    sizes = jnp.where(number % 4 == 0, named(packed, number // 4), named(common, number - number // 4 - 1))
    mixed = jax.random.permutation(jax.random.fold_in(own, 3), number_of)
    giver, sink = mixed[0:number_of // 2 * 2:2], mixed[1:number_of // 2 * 2:2]
    room = jnp.minimum(sizes[giver] - 1, bound - sizes[sink]) // 2
    room = jnp.where((giver == sequence[0]) | (sink == sequence[0]) | (sizes[sink] == 0), 0, jnp.maximum(room, 0))
    shifted = jax.random.randint(jax.random.fold_in(own, 4), (number_of // 2,), 0, 1 << 20) % (room + 1)
    sizes = sizes.at[giver].add(-shifted).at[sink].add(shifted)
    labels = jnp.searchsorted(jnp.cumsum(sizes), jnp.arange(rows * top), side="right").astype(jnp.int32)
    table = labels.reshape(top, rows).T
    table = table[jax.random.permutation(jax.random.fold_in(own, 1), rows)]
    turn = jax.random.randint(jax.random.fold_in(own, 2), (rows, 1), 0, top)
    return jnp.take_along_axis(table, (jnp.arange(top)[None, :] + turn) % top, axis=1)


def load_shares(count, total, limit, skew, full):
    portions = [(1 << 20) // math.isqrt(grade ** skew) + 1 for grade in range(1, count + 1)]
    largest = limit if full else min(limit, max(-(-total // count), total * portions[0] // sum(portions)))
    least = 1 if total - largest >= count - 1 else 0
    counts, spare = [largest] + [least] * (count - 1), total - largest - least * (count - 1)
    while spare > 0:
        free = [i for i in range(1, count) if counts[i] < largest] or [i for i in range(1, count) if counts[i] < limit]
        pool, budget = sum([portions[i] for i in free]), spare
        for i in free:
            addition = min(limit - counts[i], max(1, budget * portions[i] // pool), spare)
            counts[i] = counts[i] + addition
            spare = spare - addition
    return np.array(counts)


def bell_draw(stream_key, shape, spread, bound, cuts=(), held_as=jnp.bfloat16):
    level = block_levels(stream_key, shape, cuts, -0.22, 0.18) if cuts else 1.0
    values = jax.random.normal(stream_key, shape, jnp.float32) * spread * level
    return jnp.minimum(jnp.maximum(values, -bound), bound).astype(held_as)


def setup_inputs(seed: int = 0) -> dict:
    keys = jax.random.split(jax.random.key(seed), 15)
    layer_input = bell_draw(keys[0], (TOKENS, D), 1.0, 6.0, ((0, 16),))
    doc_lengths = draw_doc_lengths(jax.random.fold_in(keys[14], 71), 0)
    routes_keys = jax.random.split(jax.random.fold_in(keys[2], 1), TOKENS // TOK_DEV)
    routes_turns = jax.random.permutation(jax.random.fold_in(keys[2], 3), TOKENS // TOK_DEV)
    routes = jax.vmap(lambda own, number: assign_block(jax.random.fold_in(keys[2], 2), own, number, TOK_DEV, EXPERTS, TOPK, CAP, 2))(routes_keys, routes_turns).reshape((TOKENS, TOPK))
    norm1_gain = jnp.clip(1.0 + 0.1 * jax.random.normal(keys[3], (D,), jnp.float32), 0.5, 1.5).astype(jnp.bfloat16)
    w_query = bell_draw(keys[4], (D, HEADS * HEAD_DIM), D ** -0.5, 0.15625, ((1, 2),))
    w_key = bell_draw(keys[5], (D, KV_HEADS * HEAD_DIM), D ** -0.5, 0.15625, ((1, 2),))
    w_value = bell_draw(keys[6], (D, KV_HEADS * HEAD_DIM), D ** -0.5, 0.15625, ((1, 2),))
    w_out = bell_draw(keys[7], (HEADS * HEAD_DIM, D), (HEADS * HEAD_DIM // 16) ** -0.5, 0.625, ((0, 2),))
    norm2_gain = jnp.clip(1.0 + 0.1 * jax.random.normal(keys[8], (D,), jnp.float32), 0.5, 1.5).astype(jnp.bfloat16)
    w_router = bell_draw(keys[9], (D, EXPERTS), (4 * D) ** -0.5, 0.078125)
    w_gate = bell_draw(keys[10], (EXPERTS * SPLIT, D, FF // SPLIT), D ** -0.5, 0.15625, ((0, 16), (2, 2)))
    w_up = bell_draw(keys[11], (EXPERTS * SPLIT, D, FF // SPLIT), D ** -0.5, 0.15625, ((0, 16), (2, 2)))
    w_down = bell_draw(keys[12], (EXPERTS * SPLIT, FF // SPLIT, D), (FF // 8) ** -0.5, 0.75, ((0, 16), (1, 2)))
    cotangent = bell_draw(keys[13], (TOKENS, D), 1.0, 6.0, ((0, 16),))
    return dict(layer_input=layer_input, doc_lengths=doc_lengths, routes=routes, norm1_gain=norm1_gain, w_query=w_query, w_key=w_key, w_value=w_value, w_out=w_out, norm2_gain=norm2_gain, w_router=w_router, w_gate=w_gate, w_up=w_up, w_down=w_down, cotangent=cotangent)


EPSILON = 1e-06
NEGATIVE = -1e+30

@jax.custom_vjp
def low(v):
    return lax.optimization_barrier(v.astype(jnp.bfloat16)).astype(jnp.float32)

@jax.custom_vjp
def low_back(v):
    return v

def low_keep(v):
    return (low(v), None)

def low_pass(kept, grad):
    return (grad,)

def back_keep(v):
    return (v, None)

def back_low(kept, grad):
    return (low(grad),)
low.defvjp(low_keep, low_pass)
low_back.defvjp(back_keep, back_low)

def matmul(left, right):
    return jnp.dot(left, right, precision=lax.Precision.HIGHEST, preferred_element_type=jnp.float32)

def rms_norm(values, gain):
    return values * lax.rsqrt(lax.optimization_barrier(jnp.mean(values * values, axis=-1, keepdims=True)) + EPSILON) * gain

def rotate(values, cosine, sine_table):
    middle = values.shape[-1] // 2
    first_half = values[..., :middle]
    second_half = values[..., middle:]
    return jnp.concatenate([first_half * cosine - second_half * sine_table, second_half * cosine + first_half * sine_table], axis=-1)

def frequencies():
    return jnp.exp(jnp.arange(HEAD_DIM // 2, dtype=jnp.float32) * (-2.0 * math.log(10000.0) / HEAD_DIM))

def attend(inputs):
    queries, key_rows, values, segment = inputs
    raw_scores = jnp.einsum('qhgd,shd->hgqs', queries, key_rows, precision=lax.Precision.HIGHEST)
    scores = low_back(raw_scores) * HEAD_DIM ** (-0.5)
    token_index = jnp.arange(TOK_DEV, dtype=jnp.int32)
    visible = (segment[:, None] == segment[None, :]) & (token_index[:, None] >= token_index[None, :])
    scores = jnp.where(visible[None, None], scores, NEGATIVE)
    weights = low(jax.nn.softmax(scores, axis=-1))
    mixed_heads = jnp.einsum('hgqs,shd->qhgd', weights, values, precision=lax.Precision.HIGHEST)
    return low(low_back(mixed_heads))

def expert_rows(row_block, gate_e, up_e, down_e):
    block_width = FF // (SPLIT * N_TENSOR)
    running = jnp.zeros((row_block.shape[0], D), jnp.float32)
    expert_in = low_back(row_block)
    for part_id in range(SPLIT * N_TENSOR):
        column_start = part_id * block_width
        column_end = column_start + block_width
        gate_pre = low_back(matmul(expert_in, gate_e[:, column_start:column_end]))
        up_pre = low_back(matmul(expert_in, up_e[:, column_start:column_end]))
        activated = low(jax.nn.silu(gate_pre) * up_pre)
        running = running + low(matmul(activated, down_e[column_start:column_end]))
    return low_back(running)

def reference(layer_input, doc_lengths, routes, norm1_gain, w_query, w_key, w_value, w_out, norm2_gain, w_router, w_gate, w_up, w_down, cotangent):
    groups = HEADS // KV_HEADS
    token_index = jnp.arange(TOK_DEV, dtype=jnp.int32)
    seq_ends = jnp.cumsum(doc_lengths, axis=1).astype(jnp.int32)
    seq_starts = seq_ends - doc_lengths
    segment = lax.optimization_barrier(jnp.sum((token_index[None, :, None] >= seq_ends[:, None, :]).astype(jnp.int32), axis=2))
    slot_ids = jnp.arange(SEQS, dtype=jnp.int32)
    seq_first = lax.optimization_barrier(jnp.sum(jnp.where(segment[:, :, None] == slot_ids[None, None, :], seq_starts[:, None, :], 0), axis=2))
    position = (token_index[None, :] - seq_first).astype(jnp.float32).reshape(TOKENS)
    angles = position[:, None] * frequencies()[None, :]
    cosine = jnp.cos(angles)[:, None, :]
    sine_table = jnp.sin(angles)[:, None, :]
    flat_routes = routes.astype(jnp.int32).reshape(N_DP, TOK_DEV * TOPK)
    picked = (flat_routes[:, :, None] == jnp.arange(EXPERTS, dtype=jnp.int32)[None, None, :]).astype(jnp.int32)
    ranking = lax.optimization_barrier(jnp.sum(jnp.cumsum(picked, axis=1) * picked, axis=2)) - 1
    slot_index = flat_routes * (N_DP * CAP) + jnp.arange(N_DP, dtype=jnp.int32)[:, None] * CAP + ranking
    slot_flat = slot_index.reshape(-1).astype(jnp.int32)
    route_index = jnp.arange(TOKENS * TOPK, dtype=jnp.int32)
    slot_route = jnp.full((EXPERTS * N_DP * CAP,), TOKENS * TOPK, jnp.int32).at[slot_flat].set(route_index)
    slot_token = jnp.full((EXPERTS * N_DP * CAP,), TOKENS, jnp.int32).at[slot_flat].set(route_index // TOPK)
    slot_route = slot_route.reshape(EXPERTS, N_DP * CAP)
    slot_token = slot_token.reshape(EXPERTS, N_DP * CAP)

    def forward(inputs_f, gain_one, query_w, key_w, value_w, out_w, gain_two, router_w, gate_rows, up_rows, down_rows):
        gate_w = gate_rows.reshape(EXPERTS, SPLIT, D, FF // SPLIT).transpose(0, 2, 1, 3).reshape(EXPERTS, D, FF)
        up_w = up_rows.reshape(EXPERTS, SPLIT, D, FF // SPLIT).transpose(0, 2, 1, 3).reshape(EXPERTS, D, FF)
        down_w = down_rows.reshape(EXPERTS, FF, D)
        normed = low(rms_norm(inputs_f, gain_one))
        query_pre = low_back(matmul(normed, query_w)).reshape(TOKENS, HEADS, HEAD_DIM)
        queries = low(rotate(query_pre, cosine, sine_table))
        key_pre = low_back(matmul(normed, key_w)).reshape(TOKENS, KV_HEADS, HEAD_DIM)
        key_rows = low(rotate(key_pre, cosine, sine_table))
        values = low(low_back(matmul(normed, value_w))).reshape(TOKENS, KV_HEADS, HEAD_DIM)
        mixed_heads = lax.map(jax.checkpoint(attend), (queries.reshape(N_DP, TOK_DEV, KV_HEADS, groups, HEAD_DIM), key_rows.reshape(N_DP, TOK_DEV, KV_HEADS, HEAD_DIM), values.reshape(N_DP, TOK_DEV, KV_HEADS, HEAD_DIM), segment))
        attention = low_back(matmul(mixed_heads.reshape(TOKENS, HEADS * HEAD_DIM), out_w))
        hidden = inputs_f + attention
        normed_two = low(rms_norm(hidden, gain_two))
        logits = low_back(matmul(normed_two, router_w))
        chosen = jnp.take_along_axis(logits, routes.astype(jnp.int32), axis=1)
        gate_probs = jax.nn.softmax(chosen, axis=-1)
        padded_rows = jnp.concatenate([normed_two, jnp.zeros((1, D), jnp.float32)], axis=0)
        padded_gates = jnp.concatenate([gate_probs.reshape(-1), jnp.zeros((1,), jnp.float32)])

        def expert_step(running, pieces):
            token_ids, route_ids, gate_e, up_e, down_e = pieces
            row_block = padded_rows[token_ids]
            route_gate = padded_gates[route_ids]
            result = expert_rows(row_block, gate_e, up_e, down_e)
            return (running.at[token_ids].add(route_gate[:, None] * result), None)
        mixture, unused = lax.scan(jax.checkpoint(expert_step), jnp.zeros((TOKENS + 1, D), jnp.float32), (slot_token, slot_route, gate_w, up_w, down_w))
        return hidden + mixture[:TOKENS]
    output, pullback = jax.vjp(forward, layer_input.astype(jnp.float32), norm1_gain.astype(jnp.float32), w_query.astype(jnp.float32), w_key.astype(jnp.float32), w_value.astype(jnp.float32), w_out.astype(jnp.float32), norm2_gain.astype(jnp.float32), w_router.astype(jnp.float32), w_gate.astype(jnp.float32), w_up.astype(jnp.float32), w_down.astype(jnp.float32))
    grads = pullback(cotangent.astype(jnp.float32))
    return (output.astype(jnp.bfloat16), grads[0].astype(jnp.bfloat16), grads[1], grads[2], grads[3], grads[4], grads[5], grads[6], grads[7], grads[8], grads[9], grads[10])
```

```python
import functools
import math

import jax
import jax.numpy as jnp
from jax import lax
from jax.experimental import pallas as pl
from jax.experimental.pallas import tpu as pltpu
from jax.sharding import PartitionSpec as P

HEAD_DIM = 64
HEADS = 24
KV_HEADS = 8
EPSILON = 1e-06
NEGATIVE = -1e30
BF16 = jnp.bfloat16
F32 = jnp.float32
NN = (((1,), (0,)), ((), ()))
NT = (((1,), (1,)), ((), ()))
TN = (((0,), (0,)), ((), ()))
VMEM_LIMIT = 56 * 1024 * 1024


def dot(left, right, dims=NN):
    return lax.dot_general(left, right, dims, preferred_element_type=F32)


def routed_kernel(*refs):
    hn, dy = refs[0:4], refs[4:8]
    mask, onehot, router = refs[8:11]
    wg, wu, wd = refs[11:13], refs[13:15], refs[15:17]
    dx, mix = refs[17:21], refs[21:25]
    dgate, pre, act = refs[25:28]
    hbuf, dbuf, xbuf, mbuf, in_sem, out_sem = refs[28:]
    step = pl.program_id(0)
    slot = lax.rem(step, 2)

    def fetch(s, to):
        return (
            pltpu.make_async_copy(hn[s], hbuf.at[to], in_sem.at[to, 0]),
            pltpu.make_async_copy(dy[s], dbuf.at[to], in_sem.at[to, 1]),
        )

    def put(s, at):
        return (
            pltpu.make_async_copy(xbuf.at[at], dx[s], out_sem.at[at, 0]),
            pltpu.make_async_copy(mbuf.at[at], mix[s], out_sem.at[at, 1]),
        )

    @pl.when(step == 0)
    def _():
        for copy in fetch(0, 0):
            copy.start()

    for s in range(1, 4):

        @pl.when(step == s - 1)
        def _():
            for copy in fetch(s, s % 2):
                copy.start()

    for copy in fetch(0, slot):
        copy.wait()
    for s in range(2, 4):

        @pl.when(step == s)
        def _():
            for copy in put(s - 2, s % 2):
                copy.wait()

    rows = hbuf[slot]
    grads = dbuf[slot]
    logits = dot(rows, router[...], NT) + mask[...]
    weights = jnp.exp(logits - jnp.max(logits, axis=1, keepdims=True))
    gate = jnp.sum(weights * onehot[...], axis=1, keepdims=True) / jnp.sum(
        weights, axis=1, keepdims=True
    )
    width = wg[0].shape[1]
    back = mixed = gate_grad = None
    for c in range(2):
        gu = dot(rows, wg[c][...])
        up = dot(rows, wu[c][...])
        da = dot(grads, wd[c][...], NT)
        sig = 1.0 / (1.0 + jnp.exp(-gu))
        silu = gu * sig
        value = silu * up
        own = jnp.sum(value * da, axis=1, keepdims=True)
        gate_grad = own if c == 0 else gate_grad + own
        low = (value * gate).astype(BF16)
        act[:, c * width : (c + 1) * width] = low
        own = dot(low, wd[c][...])
        mixed = own if c == 0 else mixed + own
        da = da * gate
        dgu = (da * up * sig * (1.0 + gu * (1.0 - sig))).astype(BF16)
        dup = (da * silu).astype(BF16)
        pre[:, 2 * c * width : (2 * c + 1) * width] = dgu
        pre[:, (2 * c + 1) * width : (2 * c + 2) * width] = dup
        own = dot(dgu, wg[c][...], NT) + dot(dup, wu[c][...], NT)
        back = own if c == 0 else back + own
    xbuf[slot] = back.astype(BF16)
    mbuf[slot] = mixed.astype(BF16)
    dgate[...] = jnp.broadcast_to(gate_grad, dgate.shape)
    for s in range(4):

        @pl.when(step == s)
        def _():
            for copy in put(s, s % 2):
                copy.start()

    @pl.when(step == 3)
    def _():
        for copy in put(2, 0) + put(3, 1):
            copy.wait()


def routed(hn, dy, mask, onehot, router, wg, wu, wd):
    rows, model = hn[0].shape
    width = wg[0].shape[1]
    hbm = pl.BlockSpec(memory_space=pl.ANY)

    def full(array):
        return pl.BlockSpec(array.shape, lambda i: (0, 0))

    def tile(columns):
        return pl.BlockSpec((rows, columns), lambda i: (i, 0))

    out = jax.ShapeDtypeStruct
    got = pl.pallas_call(
        routed_kernel,
        grid=(4,),
        in_specs=[hbm] * 8
        + [tile(mask.shape[1]), full(onehot), full(router)]
        + [full(array) for array in (*wg, *wu, *wd)],
        out_specs=[hbm] * 8 + [tile(128), tile(4 * width), tile(2 * width)],
        out_shape=[out((rows, model), BF16)] * 8
        + [
            out((4 * rows, 128), F32),
            out((4 * rows, 4 * width), BF16),
            out((4 * rows, 2 * width), BF16),
        ],
        scratch_shapes=[pltpu.VMEM((2, rows, model), BF16)] * 4
        + [pltpu.SemaphoreType.DMA((2, 2))] * 2,
        compiler_params=pltpu.CompilerParams(vmem_limit_bytes=VMEM_LIMIT),
        cost_estimate=pl.CostEstimate(
            flops=4 * 12 * rows * model * 2 * width,
            bytes_accessed=16 * rows * model * 2,
            transcendentals=0,
        ),
        name="routed_rows",
    )(*hn, *dy, mask, onehot, router, *wg, *wu, *wd)
    return got[0:4], got[4:8], got[8], got[9], got[10]


def expert_grads_kernel(count, *refs):
    hn, dy = refs[:count], refs[count : 2 * count]
    blocks = count // 4
    pre = refs[2 * count : 2 * count + blocks]
    act = refs[2 * count + blocks : 2 * count + 2 * blocks]
    gu, gd, hbuf, dbuf, pbuf, abuf, sem = refs[2 * count + 2 * blocks :]
    step = pl.program_id(0)
    slot = lax.rem(step, 2)
    rows = hbuf.shape[1]

    def fetch(s, to):
        piece = pl.ds((s % 4) * rows, rows)
        return (
            pltpu.make_async_copy(hn[s], hbuf.at[to], sem.at[to, 0]),
            pltpu.make_async_copy(dy[s], dbuf.at[to], sem.at[to, 1]),
            pltpu.make_async_copy(pre[s // 4].at[piece], pbuf.at[to], sem.at[to, 2]),
            pltpu.make_async_copy(act[s // 4].at[piece], abuf.at[to], sem.at[to, 3]),
        )

    @pl.when(step == 0)
    def _():
        for copy in fetch(0, 0):
            copy.start()
        gu[...] = jnp.zeros_like(gu)
        gd[...] = jnp.zeros_like(gd)

    for s in range(1, count):

        @pl.when(step == s - 1)
        def _():
            for copy in fetch(s, s % 2):
                copy.start()

    for copy in fetch(0, slot):
        copy.wait()
    gu[...] += dot(hbuf[slot], pbuf[slot], TN)
    gd[...] += dot(abuf[slot], dbuf[slot], TN)


def expert_grads(hn, dy, pre, act):
    count = len(hn)
    rows, model = hn[0].shape
    four, two = pre[0].shape[1], act[0].shape[1]
    hbm = pl.BlockSpec(memory_space=pl.ANY)
    out = jax.ShapeDtypeStruct
    return pl.pallas_call(
        functools.partial(expert_grads_kernel, count),
        grid=(count,),
        in_specs=[hbm] * (2 * count + len(pre) + len(act)),
        out_specs=[
            pl.BlockSpec((model, four), lambda i: (0, 0)),
            pl.BlockSpec((two, model), lambda i: (0, 0)),
        ],
        out_shape=[out((model, four), F32), out((two, model), F32)],
        scratch_shapes=[
            pltpu.VMEM((2, rows, model), BF16),
            pltpu.VMEM((2, rows, model), BF16),
            pltpu.VMEM((2, rows, four), BF16),
            pltpu.VMEM((2, rows, two), BF16),
            pltpu.SemaphoreType.DMA((2, 4)),
        ],
        compiler_params=pltpu.CompilerParams(vmem_limit_bytes=VMEM_LIMIT),
        cost_estimate=pl.CostEstimate(
            flops=4 * count * rows * model * (four + two),
            bytes_accessed=2 * count * rows * model * 2,
            transcendentals=0,
        ),
        name="expert_grads",
    )(*hn, *dy, *pre, *act)


class Places:
    def __init__(self):
        self.count = lax.axis_size("dp")
        self.ring = self.count // 4
        me = lax.axis_index("dp")
        self.z, self.y, self.x = me // 4, (me // 2) % 2, me % 2
        self.t = lax.axis_index("tensor")

    def by_x(self, array):
        return lax.ppermute(array, "dp", [(i, i ^ 1) for i in range(self.count)])

    def by_y(self, array):
        return lax.ppermute(array, "dp", [(i, i ^ 2) for i in range(self.count)])

    def by_z(self, array):
        return lax.ppermute(array, "dp", [(i, (i + 4) % self.count) for i in range(self.count)])

    def by_t(self, array):
        return lax.ppermute(array, "tensor", [(0, 1), (1, 0)])

    def spread(self, first, second):
        near_one = jnp.concatenate([first, self.by_x(first)], axis=0)
        near_two = jnp.concatenate([second, self.by_y(second)], axis=0)
        return near_one, self.by_y(near_one), near_two, self.by_x(near_two)

    def collect(self, near_one, far_one, near_two, far_two):
        half = near_one.shape[0] // 2
        one = add(near_one, self.by_y(far_one))
        two = add(near_two, self.by_x(far_two))
        return (
            add(one[:half], self.by_x(one[half:])),
            add(two[:half], self.by_y(two[half:])),
        )

    def absolute(self, relative):
        relative = jnp.where(self.y == 1, jnp.flip(relative, 1), relative)
        relative = jnp.where(self.x == 1, jnp.flip(relative, 2), relative)
        return jnp.roll(jnp.flip(relative, 0), self.z + 1, axis=0)

    def sum_all(self, array):
        rows, columns = array.shape
        part = rows // self.count
        grid = array.reshape(self.ring, 2, 2, part, columns)
        half = columns // 2

        def split(value, place, axis):
            keep = lax.dynamic_index_in_dim(value, place, axis, keepdims=False)
            send = lax.dynamic_index_in_dim(value, 1 - place, axis, keepdims=False)
            return keep, send

        def join(own, other, place, axis):
            return jnp.where(
                place == 0, jnp.stack([own, other], axis), jnp.stack([other, own], axis)
            )

        keep, send = split(grid[..., :half], self.x, 2)
        one = add(keep, self.by_x(send))
        keep, send = split(grid[..., half:], self.y, 1)
        two = add(keep, self.by_y(send))
        keep, send = split(one, self.y, 1)
        one = add(keep, self.by_y(send))
        keep, send = split(two, self.x, 1)
        two = add(keep, self.by_x(send))
        both = jnp.concatenate([one, two], axis=-1)

        def at(j):
            return lax.dynamic_index_in_dim(both, (self.z - j) % self.ring, 0, keepdims=False)

        total = at(1 % self.ring)
        for j in range(2, self.ring + 1):
            total = add(self.by_z(total), at(j % self.ring))
        got = [total]
        for _ in range(self.ring - 1):
            got.append(self.by_z(got[-1]))
        got = jnp.stack(got)
        got = jnp.stack(
            [
                lax.dynamic_index_in_dim(got, (self.z - i) % self.ring, 0, keepdims=False)
                for i in range(self.ring)
            ]
        )
        one, two = got[..., :half], got[..., half:]
        one = join(one, self.by_y(one), self.y, 1)
        two = join(two, self.by_x(two), self.x, 1)
        one = join(one, self.by_x(one), self.x, 2)
        two = join(two, self.by_y(two), self.y, 1)
        return jnp.concatenate([one, two], axis=-1).reshape(rows, columns)

    def sum_small(self, array):
        array = array + self.by_t(array)
        step = 1
        while step < self.count:
            array = array + lax.ppermute(
                array, "dp", [(i, i ^ step) for i in range(self.count)]
            )
            step *= 2
        return array

    def own_half(self, array):
        half = array.shape[0] // 2
        return lax.dynamic_slice_in_dim(array, self.t * half, half, 0)

    def other_half(self, array):
        half = array.shape[0] // 2
        return lax.dynamic_slice_in_dim(array, (1 - self.t) * half, half, 0)

    def sum_halves(self, array):
        return self.own_half(array).astype(F32) + self.by_t(self.other_half(array)).astype(F32)

    def both_halves(self, array):
        other = self.by_t(array)
        return jnp.where(
            self.t == 0,
            jnp.concatenate([array, other], axis=0),
            jnp.concatenate([other, array], axis=0),
        )


def add(left, right):
    return (left.astype(F32) + right.astype(F32)).astype(left.dtype)


def rotate(values, cosine, sine):
    middle = values.shape[-1] // 2
    first, second = values[..., :middle], values[..., middle:]
    return jnp.concatenate(
        [first * cosine - second * sine, second * cosine + first * sine], axis=-1
    )


def frequencies():
    return jnp.exp(
        jnp.arange(HEAD_DIM // 2, dtype=F32) * (-2.0 * math.log(10000.0) / HEAD_DIM)
    )


def norm_back(values, inverse, gain, grad):
    scaled = gain * grad
    mean = jnp.mean(scaled * values, axis=-1, keepdims=True)
    return inverse * scaled - values * (inverse * inverse * inverse * mean)


def inverse_rms(values):
    return lax.rsqrt(jnp.mean(values * values, axis=-1, keepdims=True) + EPSILON)


def on_device(
    layer_input,
    doc_lengths,
    routes,
    norm1_gain,
    w_query,
    w_key,
    w_value,
    w_out,
    norm2_gain,
    w_router,
    w_gate,
    w_up,
    w_down,
    cotangent,
):
    places = Places()
    ring, count = places.ring, places.count
    tokens, model = layer_input.shape
    half = tokens // 2
    quarter = half // 2
    experts = w_router.shape[1]
    splits = count // experts
    groups = HEADS // KV_HEADS
    local_kv = w_key.shape[1] // HEAD_DIM
    scale = HEAD_DIM ** (-0.5)
    gain_one = norm1_gain.astype(F32)
    gain_two = norm2_gain.astype(F32)

    dy = places.own_half(cotangent)
    current = (dy[:quarter], dy[quarter:])
    dy_blocks = []
    for j in range(ring):
        dy_blocks.append(places.spread(*current))
        if j < ring - 1:
            current = tuple(places.by_z(piece) for piece in current)

    wg = (w_gate[0], places.by_t(w_gate[0]))
    wu = (w_up[0], places.by_t(w_up[0]))
    wd = (w_down[0], places.by_t(w_down[0]))

    lengths = doc_lengths[0]
    index = jnp.arange(tokens, dtype=jnp.int32)
    ends = jnp.cumsum(lengths)
    starts = ends - lengths
    segment = jnp.sum((index[:, None] >= ends[None, :]).astype(jnp.int32), axis=1)
    slots = jnp.arange(lengths.shape[0], dtype=jnp.int32)
    first = jnp.sum(jnp.where(segment[:, None] == slots[None, :], starts[None, :], 0), axis=1)
    angles = (index - first).astype(F32)[:, None] * frequencies()[None, :]
    cosine = jnp.cos(angles)[:, None, :]
    sine = jnp.sin(angles)[:, None, :]
    inputs = layer_input.astype(F32)
    inverse_one = inverse_rms(inputs)
    normed = (inputs * inverse_one * gain_one).astype(BF16)
    queries = rotate(dot(normed, w_query).reshape(tokens, -1, HEAD_DIM), cosine, sine)
    queries = queries.astype(BF16).reshape(tokens, local_kv, groups, HEAD_DIM)
    keys = rotate(dot(normed, w_key).reshape(tokens, local_kv, HEAD_DIM), cosine, sine)
    keys = keys.astype(BF16)
    values = dot(normed, w_value).astype(BF16).reshape(tokens, local_kv, HEAD_DIM)
    visible = (segment[:, None] == segment[None, :]) & (index[:, None] >= index[None, :])

    def scores_of():
        raw = jnp.einsum("qhgd,shd->hgqs", queries, keys, preferred_element_type=F32)
        return jnp.where(visible[None, None], raw * scale, NEGATIVE)

    scores = scores_of()
    peak = jnp.max(scores, axis=-1, keepdims=True)
    log_total = peak + jnp.log(jnp.sum(jnp.exp(scores - peak), axis=-1, keepdims=True))
    probabilities = jnp.exp(scores - log_total).astype(BF16)
    mixed_heads = jnp.einsum(
        "hgqs,shd->qhgd", probabilities, values, preferred_element_type=F32
    )
    mixed_heads = mixed_heads.astype(BF16).reshape(tokens, -1)
    attention = places.sum_halves(dot(mixed_heads, w_out).astype(BF16))
    inputs_half = places.own_half(layer_input).astype(F32)
    hidden = inputs_half + attention
    inverse_two = inverse_rms(hidden)
    normed_two = (hidden * inverse_two * gain_two).astype(BF16)

    named = jnp.any(
        places.own_half(routes)[:, :, None] == jnp.arange(experts, dtype=jnp.int32), axis=1
    )
    bits = jnp.sum(
        jnp.where(named, jnp.left_shift(1, jnp.arange(experts, dtype=jnp.int32)), 0), axis=1
    )
    bits = lax.all_to_all(
        jnp.broadcast_to(bits[None], (count, half)), "dp", split_axis=0, concat_axis=0, tiled=True
    )
    bits = places.absolute(bits.reshape(ring, 2, 2, 2, quarter))
    order = ((0, 0, 0), (0, 1, 0), (1, 0, 0), (1, 1, 0), (0, 0, 1), (1, 0, 1), (0, 1, 1), (1, 1, 1))
    lanes = jnp.arange(experts, dtype=jnp.int32)
    router_rows = w_router.T
    expert = lax.axis_index("dp") // splits
    onehot = (lanes == expert).astype(F32)[None]

    current = (normed_two[:quarter], normed_two[quarter:])
    hn_blocks = [None] * ring
    results = [None] * ring
    for j in range(ring):
        hn_blocks[j] = places.spread(*current)
        if j < ring - 1:
            current = tuple(places.by_z(piece) for piece in current)
        flags = jnp.concatenate([bits[(j, *at)] for at in order])
        mask = jnp.where(
            jnp.bitwise_and(jnp.right_shift(flags[:, None], lanes), 1) == 1, 0.0, NEGATIVE
        )
        results[j] = routed(
            hn_blocks[j], dy_blocks[j], mask, onehot, router_rows, wg, wu, wd
        )

    def home(which):
        total = None
        for step in range(1, ring + 1):
            got = places.collect(*results[step % ring][which])
            if total is None:
                total = got
            else:
                total = tuple(add(places.by_z(a), b) for a, b in zip(total, got))
        return jnp.concatenate(total, axis=0)

    normed_grad = home(0)
    gate_grads = jnp.stack(
        [results[j][2][:, 0].reshape(len(order), quarter) for j in range(ring)]
    )
    inverse_order = {at: i for i, at in enumerate(order)}
    gate_grads = jnp.stack(
        [gate_grads[:, inverse_order[(y, x, h)]] for y in (0, 1) for x in (0, 1) for h in (0, 1)],
        axis=1,
    ).reshape(ring, 2, 2, half)
    gate_grads = places.absolute(gate_grads).reshape(count, half)
    gate_grads = lax.all_to_all(gate_grads, "dp", split_axis=0, concat_axis=0, tiled=True)
    gate_grads = jnp.sum(gate_grads.reshape(experts, splits, half), axis=1).T

    logits = jnp.where(named, dot(normed_two, w_router), NEGATIVE)
    gates = jax.nn.softmax(logits, axis=-1)
    logit_grad = gates * (gate_grads - jnp.sum(gates * gate_grads, axis=-1, keepdims=True))
    logit_grad = logit_grad.astype(BF16)
    grad_router = dot(logit_grad, normed_two, TN)
    normed_grad = normed_grad.astype(F32) + dot(logit_grad, w_router, NT)
    grad_gain_two = jnp.sum(normed_grad * hidden * inverse_two, axis=0)
    hidden_grad = dy.astype(F32) + norm_back(hidden, inverse_two, gain_two, normed_grad)
    hidden_low = places.both_halves(hidden_grad.astype(BF16))
    grad_out = places.sum_all(dot(mixed_heads, hidden_low, TN).astype(BF16))

    mixed_grad = dot(hidden_low, w_out, NT).astype(BF16)
    mixed_grad = mixed_grad.reshape(tokens, local_kv, groups, HEAD_DIM)
    probabilities = jnp.exp(scores_of() - log_total)
    prob_grad = jnp.einsum("qhgd,shd->hgqs", mixed_grad, values, preferred_element_type=F32)
    balance = jnp.sum(probabilities * prob_grad, axis=-1, keepdims=True)
    score_grad = (probabilities * (prob_grad - balance) * scale).astype(BF16)
    query_grad = jnp.einsum("hgqs,shd->qhgd", score_grad, keys, preferred_element_type=F32)
    key_grad = jnp.einsum("hgqs,qhgd->shd", score_grad, queries, preferred_element_type=F32)
    value_grad = jnp.einsum(
        "hgqs,qhgd->shd", probabilities.astype(BF16), mixed_grad, preferred_element_type=F32
    )
    query_grad = rotate(query_grad.reshape(tokens, -1, HEAD_DIM), cosine, -sine)
    query_grad = query_grad.astype(BF16).reshape(tokens, -1)
    key_grad = rotate(key_grad, cosine, -sine).astype(BF16).reshape(tokens, -1)
    value_grad = value_grad.astype(BF16).reshape(tokens, -1)
    grad_heads = jnp.concatenate([query_grad, key_grad, value_grad], axis=1)
    grad_heads_w = places.sum_all(dot(normed, grad_heads, TN).astype(BF16)).astype(F32)
    normed_grad_one = (
        dot(query_grad, w_query, NT) + dot(key_grad, w_key, NT) + dot(value_grad, w_value, NT)
    )
    normed_grad_one = places.sum_halves(normed_grad_one.astype(BF16))
    inverse_half = inverse_rms(inputs_half)
    grad_gain_one = jnp.sum(normed_grad_one * inputs_half * inverse_half, axis=0)
    grad_input = hidden_grad + norm_back(inputs_half, inverse_half, gain_one, normed_grad_one)
    grad_input = places.both_halves(grad_input.astype(BF16))

    small = places.sum_small(
        jnp.concatenate([grad_router, grad_gain_one[None], grad_gain_two[None]], axis=0)
    )
    mixture = home(1).astype(F32)
    output = places.both_halves((hidden + mixture).astype(BF16))

    grad_gu = grad_d = None
    for j in range(0, ring, 4):
        span = range(j, min(j + 4, ring))
        got = expert_grads(
            [piece for i in span for piece in hn_blocks[i]],
            [piece for i in span for piece in dy_blocks[i]],
            [results[i][3] for i in span],
            [results[i][4] for i in span],
        )
        grad_gu = got[0] if grad_gu is None else grad_gu + got[0]
        grad_d = got[1] if grad_d is None else grad_d + got[1]
    width = wg[0].shape[1]
    grad_gu = grad_gu[:, : 2 * width] + places.by_t(grad_gu[:, 2 * width :])
    grad_d = grad_d[:width] + places.by_t(grad_d[width:])
    query_width, key_width = w_query.shape[1], w_key.shape[1]
    return (
        output,
        grad_input,
        small[experts],
        grad_heads_w[:, :query_width],
        grad_heads_w[:, query_width : query_width + key_width],
        grad_heads_w[:, query_width + key_width :],
        grad_out.astype(F32),
        small[experts + 1],
        small[:experts].T,
        grad_gu[None, :, :width],
        grad_gu[None, :, width:],
        grad_d[None],
    )


def solution(mesh):
    in_specs = (
        P("dp", None),
        P("dp", None),
        P("dp", None),
        P(),
        P(None, "tensor"),
        P(None, "tensor"),
        P(None, "tensor"),
        P("tensor", None),
        P(),
        P(),
        P("dp", None, "tensor"),
        P("dp", None, "tensor"),
        P("dp", "tensor", None),
        P("dp", None),
    )
    out_specs = (
        P("dp", None),
        P("dp", None),
        P(),
        P(None, "tensor"),
        P(None, "tensor"),
        P(None, "tensor"),
        P("tensor", None),
        P(),
        P(),
        P("dp", None, "tensor"),
        P("dp", None, "tensor"),
        P("dp", "tensor", None),
    )
    return jax.shard_map(
        on_device, mesh=mesh, in_specs=in_specs, out_specs=out_specs, check_vma=False
    )
```

```python
import functools
import math

import jax
import jax.numpy as jnp
from jax import lax
from jax.experimental import pallas as pl
from jax.experimental.pallas import tpu as pltpu
from jax.sharding import PartitionSpec as P

HEAD_DIM = 64
HEADS = 24
KV_HEADS = 8
EPSILON = 1e-06
NEGATIVE = -1e30
BF16 = jnp.bfloat16
F32 = jnp.float32
NN = (((1,), (0,)), ((), ()))
NT = (((1,), (1,)), ((), ()))
TN = (((0,), (0,)), ((), ()))
VMEM_LIMIT = 56 * 1024 * 1024
SMALL = pl.CostEstimate(flops=0, bytes_accessed=1024 * 1024, transcendentals=0)


def dot(left, right, dims=NN):
    return lax.dot_general(left, right, dims, preferred_element_type=F32)


LABELS = [(0, 0, 0), (0, 0, 1), (0, 1, 0), (0, 1, 1), (1, 0, 0), (1, 0, 1), (1, 1, 0), (1, 1, 1)]
SPREAD = [
    [(0, 0, 0), (0, 0, 1)],
    [(0, 1, 0), (0, 1, 1)],
    [(1, 0, 0), (1, 0, 1)],
    [(1, 1, 0)],
    [(1, 1, 1)],
]
WIDE = [(0, 0, 0), (0, 1, 0), (1, 0, 0), (1, 1, 0)]
SPLIT = [WIDE, [(0, 0, 1)], [(0, 1, 1)], [(1, 0, 1)], [(1, 1, 1)]]


def near_far(order, half):
    if order == "xy":
        return [[(0, 0, half), (0, 1, half)], [(1, 0, half), (1, 1, half)]]
    return [[(0, 0, half), (1, 0, half)], [(0, 1, half), (1, 1, half)]]


def places_of(tables):
    return {label: (a, i) for a, table in enumerate(tables) for i, label in enumerate(table)}


def piece_of(refs, where, label, rows):
    array, at = where[label]
    return refs[array].at[pl.ds(at * rows, rows)]


def routed_kernel(tables, fresh, *refs):
    counts = [len(table) for table in tables]
    groups, at = [], 2
    for size in (counts[0], counts[1], 1, 1, 1, 1, 1, 0 if fresh else 1, counts[2], 1, 1, 1, 1, 1, 6):
        groups.append(refs[at : at + size])
        at += size
    numbers, bits = refs[0], refs[1]
    hn, dy, (seed,), (router,), (wg,), (wu,), (wd,), _, dx, (wide,), (mix,), *rest = groups
    (dgate,), (pre,), (act,), scratch = rest
    hbuf, dbuf, xbuf, mbuf, in_sem, out_sem = scratch
    where = [places_of(table) for table in tables]
    rows = hbuf.shape[1] // 2
    step = pl.program_id(0)
    slot = lax.rem(step, 2)

    def fetch(s, to):
        return [
            pltpu.make_async_copy(
                piece_of(source, where[n], LABELS[2 * s + i], rows),
                buffer.at[to, pl.ds(i * rows, rows)],
                in_sem.at[to, 2 * n + i],
            )
            for n, (source, buffer) in enumerate(((hn, hbuf), (dy, dbuf)))
            for i in range(2)
        ]

    def put(s, at):
        copies = []
        for i in range(2):
            p, span = 2 * s + i, pl.ds(i * rows, rows)
            target = piece_of(dx, where[2], LABELS[p], rows)
            copies.append(
                pltpu.make_async_copy(xbuf.at[at, span], target, out_sem.at[at, i])
            )
            target = wide.at[pl.ds(s * rows, rows)]
            if i == 1:
                at_row = pl.multiple_of((numbers[p] // 2) * rows, rows)
                target = mix.at[pl.ds(at_row, rows)]
            copies.append(
                pltpu.make_async_copy(mbuf.at[at, span], target, out_sem.at[at, 2 + i])
            )
        return copies

    @pl.when(step == 0)
    def _():
        for copy in fetch(0, 0):
            copy.start()
        dgate[...] = seed[...]

    for s in range(1, 4):

        @pl.when(step == s - 1)
        def _():
            for copy in fetch(s, s % 2):
                copy.start()

    for copy in fetch(0, slot):
        copy.wait()
    for s in range(2, 4):

        @pl.when(step == s)
        def _():
            for copy in put(s - 2, s % 2):
                copy.wait()

    tokens = hbuf[slot]
    grads = dbuf[slot]
    experts = router.shape[0]
    columns = jnp.transpose(bits[...])
    lane = lax.broadcasted_iota(jnp.int32, columns.shape, 1)
    ids = [numbers[2 * step], numbers[2 * step + 1]]
    flags = jnp.concatenate(
        [jnp.sum(jnp.where(lane == i, columns, 0), axis=1, keepdims=True) for i in ids], axis=0
    )
    lane = lax.broadcasted_iota(jnp.int32, (2 * rows, experts), 1)
    named = jnp.bitwise_and(lax.shift_right_logical(flags + jnp.zeros_like(lane), lane), 1) == 1
    logits = jnp.where(named, dot(tokens, router[...], NT), NEGATIVE)
    weights = jnp.exp(logits - jnp.max(logits, axis=1, keepdims=True))
    gate = jnp.sum(jnp.where(lane == numbers[8], weights, 0.0), axis=1, keepdims=True)
    gate = gate / jnp.sum(weights, axis=1, keepdims=True)
    width = wg.shape[2]
    back = mixed = gate_grad = None
    for c in range(2):
        gu = dot(tokens, wg[c])
        up = dot(tokens, wu[c])
        da = dot(grads, wd[c], NT)
        sig = 1.0 / (1.0 + jnp.exp(-gu))
        silu = gu * sig
        value = silu * up
        own = jnp.sum(value * da, axis=1, keepdims=True)
        gate_grad = own if c == 0 else gate_grad + own
        low = (value * gate).astype(BF16)
        act[:, c * width : (c + 1) * width] = low
        own = dot(low, wd[c])
        mixed = own if c == 0 else mixed + own
        da = da * gate
        dgu = (da * up * sig * (1.0 + gu * (1.0 - sig))).astype(BF16)
        dup = (da * silu).astype(BF16)
        pre[:, 2 * c * width : (2 * c + 1) * width] = dgu
        pre[:, (2 * c + 1) * width : (2 * c + 2) * width] = dup
        own = dot(dgu, wg[c], NT) + dot(dup, wu[c], NT)
        back = own if c == 0 else back + own
    xbuf[slot] = back.astype(BF16)
    mbuf[slot] = mixed.astype(BF16)
    for i in range(2):
        piece = jnp.broadcast_to(gate_grad[i * rows : (i + 1) * rows], (rows, rows))
        dgate[pl.ds(ids[i], 1), :] = jnp.transpose(piece)[:1]
    for s in range(4):

        @pl.when(step == s)
        def _():
            for copy in put(s, s % 2):
                copy.start()

    @pl.when(step == 3)
    def _():
        for copy in put(2, 0) + put(3, 1):
            copy.wait()


def routed(numbers, bits, hn, dy, mix, seed, router, wg, wu, wd, tables):
    model = hn[0].shape[1]
    rows = bits.shape[1]
    width = wg.shape[2]
    hbm = pl.BlockSpec(memory_space=pl.ANY)

    def full(array):
        return pl.BlockSpec(array.shape, lambda i: (0,) * array.ndim)

    def tile(columns):
        return pl.BlockSpec((2 * rows, columns), lambda i: (i, 0))

    out = jax.ShapeDtypeStruct
    outs = [out((len(table) * rows, model), BF16) for table in tables[2]]
    outs.append(out((4 * rows, model), BF16))
    outs.append(out((bits.shape[0] // 2 * rows, model), BF16))
    mix = [] if mix is None else [mix]
    before = 2 + len(hn) + len(dy)
    got = pl.pallas_call(
        functools.partial(routed_kernel, tables, not mix),
        grid=(4,),
        in_specs=[pl.BlockSpec(memory_space=pltpu.SMEM), full(bits)]
        + [hbm] * (len(hn) + len(dy))
        + [full(array) for array in (seed, router, wg, wu, wd)]
        + [hbm] * len(mix),
        out_specs=[hbm] * len(outs) + [full(seed), tile(4 * width), tile(2 * width)],
        out_shape=outs
        + [
            out(seed.shape, F32),
            out((8 * rows, 4 * width), BF16),
            out((8 * rows, 2 * width), BF16),
        ],
        scratch_shapes=[pltpu.VMEM((2, 2 * rows, model), BF16)] * 4
        + [pltpu.SemaphoreType.DMA((2, 4))] * 2,
        input_output_aliases={before: len(outs)}
        | ({before + 5: len(outs) - 1} if mix else {}),
        compiler_params=pltpu.CompilerParams(vmem_limit_bytes=VMEM_LIMIT),
        cost_estimate=SMALL,
        name="routed_rows",
    )(numbers, bits, *hn, *dy, seed, router, wg, wu, wd, *mix)
    split = len(tables[2])
    return got[:split], *got[split:]


def expert_grads_kernel(tables, fresh, *refs):
    blocks = len(tables)
    at, hn, dy = 0, [], []
    for into, n in ((hn, 0), (dy, 1)):
        for table in tables:
            into.append(refs[at : at + len(table[n])])
            at += len(table[n])
    pre, act = refs[at : at + blocks], refs[at + blocks : at + 2 * blocks]
    at += 2 * blocks
    if not fresh:
        gu_before, gd_before = refs[at : at + 2]
        at += 2
    gu, gd, hbuf, dbuf, pbuf, abuf, sem = refs[at:]
    step = pl.program_id(0)
    slot = lax.rem(step, 2)
    rows = hbuf.shape[1] // 2

    def fetch(s, to):
        j, s = s // 4, s % 4
        copies = [
            pltpu.make_async_copy(
                piece_of(source[j], places_of(tables[j][n]), LABELS[2 * s + i], rows),
                buffer.at[to, pl.ds(i * rows, rows)],
                sem.at[to, 2 * n + i],
            )
            for n, (source, buffer) in enumerate(((hn, hbuf), (dy, dbuf)))
            for i in range(2)
        ]
        span = pl.ds(2 * s * rows, 2 * rows)
        return copies + [
            pltpu.make_async_copy(pre[j].at[span], pbuf.at[to], sem.at[to, 4]),
            pltpu.make_async_copy(act[j].at[span], abuf.at[to], sem.at[to, 5]),
        ]

    @pl.when(step == 0)
    def _():
        for copy in fetch(0, 0):
            copy.start()
        gu[...] = jnp.zeros_like(gu) if fresh else gu_before[...]
        gd[...] = jnp.zeros_like(gd) if fresh else gd_before[...]

    for s in range(1, 4 * blocks):

        @pl.when(step == s - 1)
        def _():
            for copy in fetch(s, s % 2):
                copy.start()

    for copy in fetch(0, slot):
        copy.wait()
    width = gu.shape[2]
    for c in range(2):
        gu[c] += dot(hbuf[slot], pbuf[slot, :, c * width : (c + 1) * width], TN)
    gd[...] += dot(abuf[slot], dbuf[slot], TN)


def expert_grads(hn, dy, pre, act, tables, before):
    blocks = len(pre)
    rows, model = pre[0].shape[0] // 8, hn[0][0].shape[1]
    four, two = pre[0].shape[1], act[0].shape[1]
    hbm = pl.BlockSpec(memory_space=pl.ANY)
    out = jax.ShapeDtypeStruct
    flat = [array for group in (*hn, *dy) for array in group]
    sums = [
        pl.BlockSpec((2, model, two), lambda i: (0, 0, 0)),
        pl.BlockSpec((two, model), lambda i: (0, 0)),
    ]
    fixed = len(flat) + 2 * blocks
    return pl.pallas_call(
        functools.partial(expert_grads_kernel, tables, not before),
        grid=(4 * blocks,),
        in_specs=[hbm] * fixed + (sums if before else []),
        out_specs=sums,
        out_shape=[out((2, model, two), F32), out((two, model), F32)],
        scratch_shapes=[
            pltpu.VMEM((2, 2 * rows, model), BF16),
            pltpu.VMEM((2, 2 * rows, model), BF16),
            pltpu.VMEM((2, 2 * rows, four), BF16),
            pltpu.VMEM((2, 2 * rows, two), BF16),
            pltpu.SemaphoreType.DMA((2, 6)),
        ],
        input_output_aliases={fixed: 0, fixed + 1: 1} if before else {},
        compiler_params=pltpu.CompilerParams(vmem_limit_bytes=VMEM_LIMIT),
        cost_estimate=SMALL,
        name="expert_grads",
    )(*flat, *pre, *act, *before)


def spin(values, cosine, sine):
    lane = lax.broadcasted_iota(jnp.int32, cosine.shape, 1) % HEAD_DIM
    parts = []
    for at in range(0, values.shape[1], 128):
        part = values[:, at : at + 128]
        other = jnp.where(
            lane < HEAD_DIM // 2,
            pltpu.roll(part, 128 - HEAD_DIM // 2, 1),
            pltpu.roll(part, HEAD_DIM // 2, 1),
        )
        parts.append(part * cosine + other * sine)
    return parts


def head(ref, rows, h):
    return ref[rows, h * HEAD_DIM : (h + 1) * HEAD_DIM]


def attend_kernel(
    x, gain, wq, wk, wv, wo, cosine, sine, seg_col, seg_row, normed, q, k, v, o, sums, part, stat
):
    tokens = x.shape[0]
    groups = HEADS // KV_HEADS
    inputs = x[...].astype(F32)
    inverse = lax.rsqrt(jnp.mean(inputs * inputs, axis=1, keepdims=True) + EPSILON)
    low = (inputs * inverse * gain[...].astype(F32)).astype(BF16)
    normed[...] = low
    for ref, weight in ((q, wq), (k, wk)):
        for i, piece in enumerate(spin(dot(low, weight[...]), cosine[...], sine[...])):
            ref[:, i * 128 : (i + 1) * 128] = piece.astype(BF16)
    v[...] = dot(low, wv[...]).astype(BF16)
    stat[...] = jnp.zeros_like(stat)
    step = tokens // 2
    for c in range(2):
        rows, seen = slice(c * step, (c + 1) * step), slice(0, (c + 1) * step)
        row_id = lax.broadcasted_iota(jnp.int32, (step, (c + 1) * step), 0) + c * step
        key_id = lax.broadcasted_iota(jnp.int32, (step, (c + 1) * step), 1)
        visible = (seg_col[rows, :] == seg_row[:, seen]) & (row_id >= key_id)
        for g in range(k.shape[1] // HEAD_DIM):
            keys, values = head(k, seen, g), head(v, seen, g)
            for h in range(g * groups, (g + 1) * groups):
                s = dot(head(q, rows, h), keys, NT) * HEAD_DIM**-0.5
                s = jnp.where(visible, s, NEGATIVE)
                peak = jnp.max(s, axis=1, keepdims=True)
                e = jnp.exp(s - peak)
                total = jnp.sum(e, axis=1, keepdims=True)
                p = (e * (1.0 / total)).astype(BF16)
                o[rows, h * HEAD_DIM : (h + 1) * HEAD_DIM] = dot(p, values).astype(BF16)
                stat[rows, h : h + 1] = peak + jnp.log(total)
    sums[...] = jnp.transpose(stat[...])[: sums.shape[0]]
    part[...] = dot(o[...], wo[...]).astype(BF16)


def attend(x, gain, wq, wk, wv, wo, cosine, sine, seg_col, seg_row):
    tokens, model = x.shape
    out = jax.ShapeDtypeStruct
    heads = wq.shape[1] // HEAD_DIM
    return pl.pallas_call(
        attend_kernel,
        out_shape=[
            out((tokens, model), BF16),
            out((tokens, wq.shape[1]), BF16),
            out((tokens, wk.shape[1]), BF16),
            out((tokens, wv.shape[1]), BF16),
            out((tokens, wq.shape[1]), BF16),
            out((-(-heads // 8) * 8, tokens), F32),
            out((tokens, model), BF16),
        ],
        scratch_shapes=[pltpu.VMEM((tokens, 128), F32)],
        compiler_params=pltpu.CompilerParams(vmem_limit_bytes=VMEM_LIMIT),
        cost_estimate=SMALL,
        name="attend",
    )(x, gain, wq, wk, wv, wo, cosine, sine, seg_col, seg_row)


def attend_back_kernel(
    dh, wq, wk, wv, wo, cosine, sine, seg_col, seg_row, normed, q, k, v, sums,
    weights, back, dout, dq, dk, dv, low,
):
    tokens = dh.shape[0]
    groups = HEADS // KV_HEADS
    scale = HEAD_DIM**-0.5
    dout[...] = dot(dh[...], wo[...], NT).astype(BF16)
    dk[...] = jnp.zeros_like(dk)
    dv[...] = jnp.zeros_like(dv)
    step = tokens // 2
    for c in range(2):
        rows, seen = slice(c * step, (c + 1) * step), slice(0, (c + 1) * step)
        key_id = lax.broadcasted_iota(jnp.int32, ((c + 1) * step, step), 0)
        row_id = lax.broadcasted_iota(jnp.int32, ((c + 1) * step, step), 1) + c * step
        visible = (seg_col[seen, :] == seg_row[:, rows]) & (row_id >= key_id)
        for g in range(k.shape[1] // HEAD_DIM):
            keys, values = head(k, seen, g), head(v, seen, g)
            key_sum = value_sum = None
            for h in range(g * groups, (g + 1) * groups):
                query, grad = head(q, rows, h), head(dout, rows, h)
                s = jnp.where(visible, dot(keys, query, NT) * scale, NEGATIVE)
                p = jnp.exp(s - sums[h : h + 1, rows])
                dp = dot(values, grad, NT)
                balance = jnp.sum(p * dp, axis=0, keepdims=True)
                ds = (p * (dp - balance) * scale).astype(BF16)
                dq[rows, h * HEAD_DIM : (h + 1) * HEAD_DIM] = dot(ds, keys, TN)
                own = dot(ds, query)
                key_sum = own if key_sum is None else key_sum + own
                own = dot(p.astype(BF16), grad)
                value_sum = own if value_sum is None else value_sum + own
            dk[seen, g * HEAD_DIM : (g + 1) * HEAD_DIM] += key_sum
            dv[seen, g * HEAD_DIM : (g + 1) * HEAD_DIM] += value_sum
    at = 0
    for ref in (dq, dk):
        for piece in spin(ref[...], cosine[...], -sine[...]):
            low[:, at : at + 128] = piece.astype(BF16)
            at += 128
    low[:, at:] = dv[...].astype(BF16)
    one, two = wq.shape[1], wq.shape[1] + wk.shape[1]
    total = dot(low[:, :one], wq[...], NT) + dot(low[:, one:two], wk[...], NT)
    back[...] = (total + dot(low[:, two:], wv[...], NT)).astype(BF16)
    weights[...] = dot(normed[...], low[...], TN).astype(BF16)


def attend_back(dh, wq, wk, wv, wo, cosine, sine, seg_col, seg_row, normed, q, k, v, sums):
    tokens, model = dh.shape
    out = jax.ShapeDtypeStruct
    columns = wq.shape[1] + wk.shape[1] + wv.shape[1]
    return pl.pallas_call(
        attend_back_kernel,
        out_shape=[out((model, columns), BF16), out((tokens, model), BF16)],
        scratch_shapes=[
            pltpu.VMEM((tokens, wq.shape[1]), BF16),
            pltpu.VMEM((tokens, wq.shape[1]), F32),
            pltpu.VMEM((tokens, wk.shape[1]), F32),
            pltpu.VMEM((tokens, wk.shape[1]), F32),
            pltpu.VMEM((tokens, columns), BF16),
        ],
        compiler_params=pltpu.CompilerParams(vmem_limit_bytes=VMEM_LIMIT),
        cost_estimate=SMALL,
        name="attend_back",
    )(dh, wq, wk, wv, wo, cosine, sine, seg_col, seg_row, normed, q, k, v, sums)


class Places:
    def __init__(self):
        self.count = lax.axis_size("dp")
        self.ring = self.count // 4
        me = lax.axis_index("dp")
        self.z, self.y, self.x = me // 4, (me // 2) % 2, me % 2
        self.t = lax.axis_index("tensor")
        self.sent = {"x": [], "y": [], "z": []}
        self.after = None

    def send(self, axis, array, pairs):
        sent = self.sent[axis]
        first = sent[-2:-1]
        if self.after is not None:
            first.append(self.after)
        if first:
            array = lax.optimization_barrier((array, *first))[0]
        got = lax.ppermute(array, "dp", pairs)
        sent.append(got)
        return got

    def by_x(self, array):
        return self.send("x", array, [(i, i ^ 1) for i in range(self.count)])

    def by_y(self, array):
        return self.send("y", array, [(i, i ^ 2) for i in range(self.count)])

    def by_z(self, array, step=1):
        return self.send(
            "z", array, [(i, (i + 4 * step) % self.count) for i in range(self.count)]
        )

    def by_ring(self, array, step):
        return lax.ppermute(
            array, "dp", [(i, (i + 4 * step) % self.count) for i in range(self.count)]
        )

    def by_t(self, array):
        return lax.ppermute(array, "tensor", [(0, 1), (1, 0)])

    def by(self, axis, array):
        return self.by_x(array) if axis == "x" else self.by_y(array)

    def spread_near(self, block):
        return block, self.by_x(block), self.by_y(block)

    def spread_far(self, own, beside_x, beside_y):
        half = own.shape[0] // 2
        return (
            own, beside_x, beside_y, self.by_y(beside_x[:half]), self.by_x(beside_y[half:])
        )

    def collect_far(self, near, far, order):
        return add(near, self.by(order[1], far))

    def collect_near(self, near, order):
        half = near.shape[0] // 2
        return add(near[:half], self.by(order[0], near[half:]))

    def number(self, j, label):
        y, x, half = label
        device = ((self.z - j) % self.ring) * 4 + (self.y ^ y) * 2 + (self.x ^ x)
        return device * 2 + half

    def sum_all(self, array):
        rows, columns = array.shape
        part = rows // self.count
        grid = array.reshape(self.ring, 2, 2, part, columns)
        half = columns // 2

        def split(value, place, axis):
            keep = lax.dynamic_index_in_dim(value, place, axis, keepdims=False)
            send = lax.dynamic_index_in_dim(value, 1 - place, axis, keepdims=False)
            return keep, send

        def join(own, other, place, axis):
            return jnp.where(
                place == 0, jnp.stack([own, other], axis), jnp.stack([other, own], axis)
            )

        keep_one, one = split(grid[..., :half], self.x, 2)
        keep_two, two = split(grid[..., half:], self.y, 1)
        one, two = add(keep_one, self.by_x(one)), add(keep_two, self.by_y(two))
        yield one
        keep_one, one = split(one, self.y, 1)
        keep_two, two = split(two, self.x, 1)
        got = self.by_y(one), self.by_x(two)
        one, two = add(keep_one, got[0]), add(keep_two, got[1])
        both = jnp.concatenate([one, two], axis=-1)
        yield got[0]

        def at(j):
            return lax.dynamic_index_in_dim(both, (self.z - j) % self.ring, 0, keepdims=False)

        got = [self.by_ring(at(j), -j) for j in range(1, self.ring)]
        total = sum((value.astype(F32) for value in got), at(0).astype(F32)).astype(BF16)
        got = [total]
        for j in range(1, self.ring):
            got.append(self.by_ring(total, j))
        got = jnp.stack(got)
        got = jnp.stack(
            [
                lax.dynamic_index_in_dim(got, (self.z - i) % self.ring, 0, keepdims=False)
                for i in range(self.ring)
            ]
        )
        one, two = got[..., :half], got[..., half:]
        yield
        other_one, other_two = self.by_y(one), self.by_x(two)
        one, two = join(one, other_one, self.y, 1), join(two, other_two, self.x, 1)
        yield
        other_one, other_two = self.by_x(one), self.by_y(two)
        one, two = join(one, other_one, self.x, 2), join(two, other_two, self.y, 1)
        yield jnp.concatenate([one, two], axis=-1).reshape(rows, columns)

    def own_half(self, array):
        half = array.shape[0] // 2
        return lax.dynamic_slice_in_dim(array, self.t * half, half, 0)

    def other_half(self, array):
        half = array.shape[0] // 2
        return lax.dynamic_slice_in_dim(array, (1 - self.t) * half, half, 0)

    def sum_halves(self, array):
        return self.own_half(array).astype(F32) + self.by_t(self.other_half(array)).astype(F32)

    def both_halves(self, array):
        other = self.by_t(array)
        return jnp.where(
            self.t == 0,
            jnp.concatenate([array, other], axis=0),
            jnp.concatenate([other, array], axis=0),
        )


def add(left, right):
    return (left.astype(F32) + right.astype(F32)).astype(left.dtype)


def frequencies():
    index = jnp.arange(128) % (HEAD_DIM // 2)
    return jnp.exp(index.astype(F32) * (-2.0 * math.log(10000.0) / HEAD_DIM))


def norm_back(values, inverse, gain, grad):
    scaled = gain * grad
    mean = jnp.mean(scaled * values, axis=-1, keepdims=True)
    return inverse * scaled - values * (inverse * inverse * inverse * mean)


def inverse_rms(values):
    return lax.rsqrt(jnp.mean(values * values, axis=-1, keepdims=True) + EPSILON)


def on_device(
    layer_input,
    doc_lengths,
    routes,
    norm1_gain,
    w_query,
    w_key,
    w_value,
    w_out,
    norm2_gain,
    w_router,
    w_gate,
    w_up,
    w_down,
    cotangent,
):
    places = Places()
    ring, count = places.ring, places.count
    tokens, model = layer_input.shape
    half = tokens // 2
    quarter = half // 2
    experts = w_router.shape[1]
    splits = count // experts
    gain_one = norm1_gain.astype(F32)
    gain_two = norm2_gain.astype(F32)

    dy = places.own_half(cotangent)
    block = places.spread_near(dy)
    ring_piece = dy[quarter:]
    pieces = [places.by_z(ring_piece)]
    block = places.spread_far(*block)
    wide = jnp.concatenate([piece[:quarter] for piece in block[:4]], axis=0)
    dy_second = [tuple(block[i][quarter:] for i in range(3)) + (block[4],)]
    for j in range(1, ring):
        if j + 1 < ring:
            pieces.append(places.by_z(pieces[-1]))
        beside = places.by_x(pieces[j - 1]), places.by_y(pieces[j - 1])
        far = places.by_y(beside[0]) if j % 2 else places.by_x(beside[1])
        dy_second.append((pieces[j - 1], *beside, far))
    dy_first = [wide, places.by_z(wide)]

    wg = lax.all_gather(w_gate[0], "tensor")
    wu = lax.all_gather(w_up[0], "tensor")
    wd = lax.all_gather(w_down[0], "tensor")

    lengths = doc_lengths[0]
    index = jnp.arange(tokens, dtype=jnp.int32)
    ends = jnp.cumsum(lengths)
    starts = ends - lengths
    segment = jnp.sum((index[:, None] >= ends[None, :]).astype(jnp.int32), axis=1)
    slots = jnp.arange(lengths.shape[0], dtype=jnp.int32)
    first = jnp.sum(jnp.where(segment[:, None] == slots[None, :], starts[None, :], 0), axis=1)
    angles = (index - first).astype(F32)[:, None] * frequencies()[None, :]
    cosine = jnp.cos(angles)
    sine = jnp.sin(angles) * jnp.where(jnp.arange(128) % HEAD_DIM < HEAD_DIM // 2, -1.0, 1.0)
    around = (cosine, sine, segment[:, None], segment[None, :])
    normed, queries, keys, values, mixed_heads, sums, part = attend(
        layer_input, norm1_gain[None], w_query, w_key, w_value, w_out, *around
    )
    attention = places.sum_halves(part)
    inputs_half = places.own_half(layer_input).astype(F32)
    hidden = inputs_half + attention
    inverse_two = inverse_rms(hidden)
    normed_two = (hidden * inverse_two * gain_two).astype(BF16)

    named = jnp.any(
        places.own_half(routes)[:, :, None] == jnp.arange(experts, dtype=jnp.int32), axis=1
    )
    bits = jnp.sum(
        jnp.where(named, jnp.left_shift(1, jnp.arange(experts, dtype=jnp.int32)), 0), axis=1
    )
    bits = lax.all_to_all(
        jnp.broadcast_to(bits[None], (count, half)), "dp", split_axis=0, concat_axis=0, tiled=True
    ).reshape(2 * count, quarter)
    router_rows = w_router.T
    expert = lax.axis_index("dp") // splits
    gate_grads = jnp.zeros((2 * count, quarter), F32)

    tables = (SPREAD, SPLIT, near_far("xy", 0) + near_far("yx", 1))
    dy_blocks, results, kept = [], [], []

    def run(j):
        numbers = jnp.stack([places.number(j, label) for label in LABELS] + [expert])
        dy_blocks.append((dy_first[j], *dy_second[j]))
        mix, seed = results[-1][2:4] if results else (None, gate_grads)
        results.append(
            routed(
                numbers.astype(jnp.int32), bits, hn_blocks[j], dy_blocks[j], mix, seed, router_rows,
                wg, wu, wd, tables,
            )
        )
        places.after = results[-1][3]
        kept.append(results[-1][4:6])

    def near(j):
        hn_blocks[j] = places.spread_near(ring_blocks[j])

    def far(j):
        hn_blocks[j] = places.spread_far(*hn_blocks[j])

    def back_far(j):
        parts = results[j][0]
        back[j] = [
            places.collect_far(*parts[0:2], "xy"), places.collect_far(*parts[2:4], "yx")
        ]

    def back_near(j):
        parts = [places.collect_near(part, order) for part, order in zip(back[j], ("xy", "yx"))]
        back[j] = jnp.concatenate(parts, axis=0)

    def back_ring(j):
        back[j] = places.by_z(back[j], -j)

    def onward(running, value):
        return value if running is None else add(places.by_z(running), value)

    def grads_of(blocks, before):
        per = 2 if ring < 8 else 4
        for at in range(0, len(blocks), per):
            span = blocks[at : at + per]
            before = expert_grads(
                [hn_blocks[i] for i in span],
                [dy_blocks[i] for i in span],
                [kept[i][0] for i in span],
                [kept[i][1] for i in span],
                [tables[:2] for i in span],
                before,
            )
        return before

    ring_blocks = [normed_two, places.by_z(normed_two)]
    hn_blocks, back = [None] * ring, [None] * ring
    near(0)
    near(1)
    far(0)
    for j in range(ring):
        if j + 2 < ring:
            ring_blocks.append(places.by_z(ring_blocks[-1]))
            dy_first.append(places.by_z(dy_first[-1]))
            near(j + 2)
        if j + 1 < ring:
            far(j + 1)
        if j == 3:
            first = places.by_z(results[1][1])
        if j > 2:
            back_near(j - 2)
            back_ring(j - 2)
        if j > 1:
            back_far(j - 1)
        run(j)
    last = ring - 1
    places.after = None
    back_far(last)
    if last > 1:
        back_near(last - 1)
        back_ring(last - 1)
    kept[: ring // 2] = lax.optimization_barrier((kept[: ring // 2], results[last][3]))[0]
    expert_sums = grads_of(range(ring // 2), ())
    places.after = expert_sums[1]
    back_near(last)
    places.after = None
    for j in range(2, last):
        first = places.by_z(add(first, results[j][1]))
    back_ring(last)
    moved = first
    back_far(0)
    kept[ring // 2 :] = lax.optimization_barrier((kept[ring // 2 :], back[last]))[0]
    expert_sums = grads_of(range(ring // 2, ring), expert_sums)
    back_near(0)
    second = lax.optimization_barrier((results[-1][2], back[last]))[0]
    second = lax.psum_scatter(second, "dp", scatter_dimension=0, tiled=True)
    normed_grad = sum(part.astype(F32) for part in back)
    gate_grads = lax.all_to_all(
        results[-1][3].reshape(count, half), "dp", split_axis=0, concat_axis=0, tiled=True
    )
    gate_grads = jnp.sum(gate_grads.reshape(experts, splits, half), axis=1).T

    logits = jnp.where(named, dot(normed_two, w_router), NEGATIVE)
    gates = jax.nn.softmax(logits, axis=-1)
    logit_grad = gates * (gate_grads - jnp.sum(gates * gate_grads, axis=-1, keepdims=True))
    logit_grad = logit_grad.astype(BF16)
    grad_router = dot(logit_grad, normed_two, TN)
    normed_grad = normed_grad + dot(logit_grad, w_router, NT)
    grad_gain_two = jnp.sum(normed_grad * hidden * inverse_two, axis=0)
    hidden_grad = dy.astype(F32) + norm_back(hidden, inverse_two, gain_two, normed_grad)
    hidden_low = places.both_halves(hidden_grad.astype(BF16))
    hidden_low = lax.optimization_barrier((hidden_low, moved, expert_sums[1]))[0]
    moved = places.by_z(add(moved, results[last][1]))
    first = add(moved, results[0][1])
    grad_out = dot(mixed_heads, hidden_low, TN).astype(BF16)

    grad_heads_w, part = attend_back(
        hidden_low, w_query, w_key, w_value, w_out, *around, normed, queries, keys, values, sums
    )
    grad_heads_w = places.sum_all(grad_heads_w)
    places.after = moved
    next(grad_heads_w)
    places.after = None
    first = places.collect_far(first[:half], first[half:], "xy")
    first = places.collect_near(first, "xy")
    normed_grad_one = places.sum_halves(part)
    inverse_half = inverse_rms(inputs_half)
    grad_gain_one = jnp.sum(normed_grad_one * inputs_half * inverse_half, axis=0)
    grad_input = hidden_grad + norm_back(inputs_half, inverse_half, gain_one, normed_grad_one)
    grad_input = places.both_halves(grad_input.astype(BF16))

    small = jnp.concatenate([grad_router, grad_gain_one[None], grad_gain_two[None]], axis=0)
    small = (small + places.by_t(small)).astype(BF16)
    rows, columns = grad_out.shape
    spare = 256 * (-(-small.size // (256 * rows)))
    small = jnp.pad(small.reshape(-1), (0, rows * spare - small.size)).reshape(rows, spare)
    grad_out = places.sum_all(jnp.concatenate([grad_out, small], axis=1))
    next(grad_out)
    next(grad_heads_w)
    next(grad_out)
    next(grad_heads_w)
    next(grad_out)
    next(grad_heads_w)
    next(grad_out)
    mixture = jnp.concatenate([first, second], axis=0).astype(F32)
    grad_heads_w = next(grad_heads_w).astype(F32)
    grad_out = next(grad_out).astype(F32)
    small = grad_out[:, columns:].reshape(-1)[: (experts + 2) * model].reshape(-1, model)
    grad_out = grad_out[:, :columns]
    output = places.both_halves((hidden + mixture).astype(BF16))

    grad_gu = lax.psum_scatter(expert_sums[0], "tensor", scatter_dimension=0)
    grad_d = lax.psum_scatter(expert_sums[1], "tensor", scatter_dimension=0, tiled=True)
    width = w_gate.shape[2]
    query_width, key_width = w_query.shape[1], w_key.shape[1]
    return (
        output,
        grad_input,
        small[experts],
        grad_heads_w[:, :query_width],
        grad_heads_w[:, query_width : query_width + key_width],
        grad_heads_w[:, query_width + key_width :],
        grad_out,
        small[experts + 1],
        small[:experts].T,
        grad_gu[None, :, :width],
        grad_gu[None, :, width:],
        grad_d[None],
    )


def solution(mesh):
    in_specs = (
        P("dp", None),
        P("dp", None),
        P("dp", None),
        P(),
        P(None, "tensor"),
        P(None, "tensor"),
        P(None, "tensor"),
        P("tensor", None),
        P(),
        P(),
        P("dp", None, "tensor"),
        P("dp", None, "tensor"),
        P("dp", "tensor", None),
        P("dp", None),
    )
    out_specs = (
        P("dp", None),
        P("dp", None),
        P(),
        P(None, "tensor"),
        P(None, "tensor"),
        P(None, "tensor"),
        P("tensor", None),
        P(),
        P(),
        P("dp", None, "tensor"),
        P("dp", None, "tensor"),
        P("dp", "tensor", None),
    )
    return jax.shard_map(
        on_device, mesh=mesh, in_specs=in_specs, out_specs=out_specs, check_vma=False
    )
```

```python
import functools
import math

import jax
import jax.numpy as jnp
from jax import lax
from jax.experimental import pallas as pl
from jax.experimental.pallas import tpu as pltpu
from jax.sharding import PartitionSpec as P

HEAD_DIM = 64
HEADS = 24
KV_HEADS = 8
EPSILON = 1e-06
NEGATIVE = -1e30
BF16 = jnp.bfloat16
F32 = jnp.float32
NN = (((1,), (0,)), ((), ()))
NT = (((1,), (1,)), ((), ()))
TN = (((0,), (0,)), ((), ()))
VMEM_LIMIT = 56 * 1024 * 1024
SMALL = pl.CostEstimate(flops=0, bytes_accessed=1024 * 1024, transcendentals=0)


def dot(left, right, dims=NN):
    return lax.dot_general(left, right, dims, preferred_element_type=F32)


LABELS = [(0, 0, 0), (0, 0, 1), (0, 1, 0), (0, 1, 1), (1, 0, 0), (1, 0, 1), (1, 1, 0), (1, 1, 1)]
SPREAD = [
    [(0, 0, 0), (0, 0, 1)],
    [(0, 1, 0), (0, 1, 1)],
    [(1, 0, 0), (1, 0, 1)],
    [(1, 1, 0)],
    [(1, 1, 1)],
]
WIDE = [(0, 0, 0), (0, 1, 0), (1, 0, 0), (1, 1, 0)]
SPLIT = [WIDE, [(0, 0, 1)], [(0, 1, 1)], [(1, 0, 1)], [(1, 1, 1)]]


def near_far(order, half):
    if order == "xy":
        return [[(0, 0, half), (0, 1, half)], [(1, 0, half), (1, 1, half)]]
    return [[(0, 0, half), (1, 0, half)], [(0, 1, half), (1, 1, half)]]


def places_of(tables):
    return {label: (a, i) for a, table in enumerate(tables) for i, label in enumerate(table)}


def piece_of(refs, where, label, rows):
    array, at = where[label]
    return refs[array].at[pl.ds(at * rows, rows)]


def routed_kernel(tables, fresh, *refs):
    counts = [len(table) for table in tables]
    groups, at = [], 2
    for size in (counts[0], counts[1], 1, 1, 1, 1, 1, 0 if fresh else 1, counts[2], 1, 1, 1, 1, 6):
        groups.append(refs[at : at + size])
        at += size
    numbers, bits = refs[0], refs[1]
    hn, dy, (seed,), (router,), (wg,), (wu,), (wd,), _, dx, (mix,), *rest = groups
    (dgate,), (pre,), (act,), scratch = rest
    hbuf, dbuf, xbuf, mbuf, in_sem, out_sem = scratch
    where = [places_of(table) for table in tables]
    rows = hbuf.shape[1] // 2
    step = pl.program_id(0)
    slot = lax.rem(step, 2)

    def fetch(s, to):
        return [
            pltpu.make_async_copy(
                piece_of(source, where[n], LABELS[2 * s + i], rows),
                buffer.at[to, pl.ds(i * rows, rows)],
                in_sem.at[to, 2 * n + i],
            )
            for n, (source, buffer) in enumerate(((hn, hbuf), (dy, dbuf)))
            for i in range(2)
        ]

    def put(s, at):
        copies = []
        for i in range(2):
            p, span = 2 * s + i, pl.ds(i * rows, rows)
            target = piece_of(dx, where[2], LABELS[p], rows)
            copies.append(
                pltpu.make_async_copy(xbuf.at[at, span], target, out_sem.at[at, i])
            )
            target = mix.at[pl.ds(pl.multiple_of(numbers[p] * rows, rows), rows)]
            copies.append(
                pltpu.make_async_copy(mbuf.at[at, span], target, out_sem.at[at, 2 + i])
            )
        return copies

    @pl.when(step == 0)
    def _():
        for copy in fetch(0, 0):
            copy.start()
        dgate[...] = seed[...]

    for s in range(1, 4):

        @pl.when(step == s - 1)
        def _():
            for copy in fetch(s, s % 2):
                copy.start()

    for copy in fetch(0, slot):
        copy.wait()
    for s in range(2, 4):

        @pl.when(step == s)
        def _():
            for copy in put(s - 2, s % 2):
                copy.wait()

    tokens = hbuf[slot]
    grads = dbuf[slot]
    experts = router.shape[0]
    columns = jnp.transpose(bits[...])
    lane = lax.broadcasted_iota(jnp.int32, columns.shape, 1)
    ids = [numbers[2 * step], numbers[2 * step + 1]]
    flags = jnp.concatenate(
        [jnp.sum(jnp.where(lane == i, columns, 0), axis=1, keepdims=True) for i in ids], axis=0
    )
    lane = lax.broadcasted_iota(jnp.int32, (2 * rows, experts), 1)
    named = jnp.bitwise_and(lax.shift_right_logical(flags + jnp.zeros_like(lane), lane), 1) == 1
    logits = jnp.where(named, dot(tokens, router[...], NT), NEGATIVE)
    weights = jnp.exp(logits - jnp.max(logits, axis=1, keepdims=True))
    gate = jnp.sum(jnp.where(lane == numbers[8], weights, 0.0), axis=1, keepdims=True)
    gate = gate / jnp.sum(weights, axis=1, keepdims=True)
    width = wg.shape[2]
    back = mixed = gate_grad = None
    for c in range(2):
        gu = dot(tokens, wg[c])
        up = dot(tokens, wu[c])
        da = dot(grads, wd[c], NT)
        sig = 1.0 / (1.0 + jnp.exp(-gu))
        silu = gu * sig
        value = silu * up
        own = jnp.sum(value * da, axis=1, keepdims=True)
        gate_grad = own if c == 0 else gate_grad + own
        low = (value * gate).astype(BF16)
        act[:, c * width : (c + 1) * width] = low
        own = dot(low, wd[c])
        mixed = own if c == 0 else mixed + own
        da = da * gate
        dgu = (da * up * sig * (1.0 + gu * (1.0 - sig))).astype(BF16)
        dup = (da * silu).astype(BF16)
        pre[:, 2 * c * width : (2 * c + 1) * width] = dgu
        pre[:, (2 * c + 1) * width : (2 * c + 2) * width] = dup
        own = dot(dgu, wg[c], NT) + dot(dup, wu[c], NT)
        back = own if c == 0 else back + own
    xbuf[slot] = back.astype(BF16)
    mbuf[slot] = mixed.astype(BF16)
    for i in range(2):
        piece = jnp.broadcast_to(gate_grad[i * rows : (i + 1) * rows], (rows, rows))
        dgate[pl.ds(ids[i], 1), :] = jnp.transpose(piece)[:1]
    for s in range(4):

        @pl.when(step == s)
        def _():
            for copy in put(s, s % 2):
                copy.start()

    @pl.when(step == 3)
    def _():
        for copy in put(2, 0) + put(3, 1):
            copy.wait()


def routed(numbers, bits, hn, dy, mix, seed, router, wg, wu, wd, tables):
    model = hn[0].shape[1]
    rows = bits.shape[1]
    width = wg.shape[2]
    hbm = pl.BlockSpec(memory_space=pl.ANY)

    def full(array):
        return pl.BlockSpec(array.shape, lambda i: (0,) * array.ndim)

    def tile(columns):
        return pl.BlockSpec((2 * rows, columns), lambda i: (i, 0))

    out = jax.ShapeDtypeStruct
    outs = [out((len(table) * rows, model), BF16) for table in tables[2]]
    outs.append(out((bits.shape[0] * rows, model), BF16))
    mix = [] if mix is None else [mix]
    before = 2 + len(hn) + len(dy)
    got = pl.pallas_call(
        functools.partial(routed_kernel, tables, not mix),
        grid=(4,),
        in_specs=[pl.BlockSpec(memory_space=pltpu.SMEM), full(bits)]
        + [hbm] * (len(hn) + len(dy))
        + [full(array) for array in (seed, router, wg, wu, wd)]
        + [hbm] * len(mix),
        out_specs=[hbm] * len(outs) + [full(seed), tile(4 * width), tile(2 * width)],
        out_shape=outs
        + [
            out(seed.shape, F32),
            out((8 * rows, 4 * width), BF16),
            out((8 * rows, 2 * width), BF16),
        ],
        scratch_shapes=[pltpu.VMEM((2, 2 * rows, model), BF16)] * 4
        + [pltpu.SemaphoreType.DMA((2, 4))] * 2,
        input_output_aliases={before: len(outs)}
        | ({before + 5: len(outs) - 1} if mix else {}),
        compiler_params=pltpu.CompilerParams(vmem_limit_bytes=VMEM_LIMIT),
        cost_estimate=SMALL,
        name="routed_rows",
    )(numbers, bits, *hn, *dy, seed, router, wg, wu, wd, *mix)
    split = len(tables[2])
    return got[:split], *got[split:]


def expert_grads_kernel(tables, fresh, *refs):
    blocks = len(tables)
    at, hn, dy = 0, [], []
    for into, n in ((hn, 0), (dy, 1)):
        for table in tables:
            into.append(refs[at : at + len(table[n])])
            at += len(table[n])
    pre, act = refs[at : at + blocks], refs[at + blocks : at + 2 * blocks]
    at += 2 * blocks
    if not fresh:
        gu_before, gd_before = refs[at : at + 2]
        at += 2
    gu, gd, hbuf, dbuf, pbuf, abuf, sem = refs[at:]
    step = pl.program_id(0)
    slot = lax.rem(step, 2)
    rows = hbuf.shape[1] // 2

    def fetch(s, to):
        j, s = s // 4, s % 4
        copies = [
            pltpu.make_async_copy(
                piece_of(source[j], places_of(tables[j][n]), LABELS[2 * s + i], rows),
                buffer.at[to, pl.ds(i * rows, rows)],
                sem.at[to, 2 * n + i],
            )
            for n, (source, buffer) in enumerate(((hn, hbuf), (dy, dbuf)))
            for i in range(2)
        ]
        span = pl.ds(2 * s * rows, 2 * rows)
        return copies + [
            pltpu.make_async_copy(pre[j].at[span], pbuf.at[to], sem.at[to, 4]),
            pltpu.make_async_copy(act[j].at[span], abuf.at[to], sem.at[to, 5]),
        ]

    @pl.when(step == 0)
    def _():
        for copy in fetch(0, 0):
            copy.start()
        gu[...] = jnp.zeros_like(gu) if fresh else gu_before[...]
        gd[...] = jnp.zeros_like(gd) if fresh else gd_before[...]

    for s in range(1, 4 * blocks):

        @pl.when(step == s - 1)
        def _():
            for copy in fetch(s, s % 2):
                copy.start()

    for copy in fetch(0, slot):
        copy.wait()
    width = gu.shape[2]
    for c in range(2):
        gu[c] += dot(hbuf[slot], pbuf[slot, :, c * width : (c + 1) * width], TN)
    gd[...] += dot(abuf[slot], dbuf[slot], TN)


def expert_grads(hn, dy, pre, act, tables, before):
    blocks = len(pre)
    rows, model = pre[0].shape[0] // 8, hn[0][0].shape[1]
    four, two = pre[0].shape[1], act[0].shape[1]
    hbm = pl.BlockSpec(memory_space=pl.ANY)
    out = jax.ShapeDtypeStruct
    flat = [array for group in (*hn, *dy) for array in group]
    sums = [
        pl.BlockSpec((2, model, two), lambda i: (0, 0, 0)),
        pl.BlockSpec((two, model), lambda i: (0, 0)),
    ]
    fixed = len(flat) + 2 * blocks
    return pl.pallas_call(
        functools.partial(expert_grads_kernel, tables, not before),
        grid=(4 * blocks,),
        in_specs=[hbm] * fixed + (sums if before else []),
        out_specs=sums,
        out_shape=[out((2, model, two), F32), out((two, model), F32)],
        scratch_shapes=[
            pltpu.VMEM((2, 2 * rows, model), BF16),
            pltpu.VMEM((2, 2 * rows, model), BF16),
            pltpu.VMEM((2, 2 * rows, four), BF16),
            pltpu.VMEM((2, 2 * rows, two), BF16),
            pltpu.SemaphoreType.DMA((2, 6)),
        ],
        input_output_aliases={fixed: 0, fixed + 1: 1} if before else {},
        compiler_params=pltpu.CompilerParams(vmem_limit_bytes=VMEM_LIMIT),
        cost_estimate=SMALL,
        name="expert_grads",
    )(*flat, *pre, *act, *before)


def spin(values, cosine, sine):
    lane = lax.broadcasted_iota(jnp.int32, cosine.shape, 1) % HEAD_DIM
    parts = []
    for at in range(0, values.shape[1], 128):
        part = values[:, at : at + 128]
        other = jnp.where(
            lane < HEAD_DIM // 2,
            pltpu.roll(part, 128 - HEAD_DIM // 2, 1),
            pltpu.roll(part, HEAD_DIM // 2, 1),
        )
        parts.append(part * cosine + other * sine)
    return parts


def head(ref, rows, h):
    return ref[rows, h * HEAD_DIM : (h + 1) * HEAD_DIM]


def attend_kernel(
    x, gain, wq, wk, wv, wo, cosine, sine, seg_col, seg_row, normed, q, k, v, o, sums, part, stat
):
    tokens = x.shape[0]
    groups = HEADS // KV_HEADS
    inputs = x[...].astype(F32)
    inverse = lax.rsqrt(jnp.mean(inputs * inputs, axis=1, keepdims=True) + EPSILON)
    low = (inputs * inverse * gain[...].astype(F32)).astype(BF16)
    normed[...] = low
    for ref, weight in ((q, wq), (k, wk)):
        for i, piece in enumerate(spin(dot(low, weight[...]), cosine[...], sine[...])):
            ref[:, i * 128 : (i + 1) * 128] = piece.astype(BF16)
    v[...] = dot(low, wv[...]).astype(BF16)
    stat[...] = jnp.zeros_like(stat)
    step = tokens // 2
    for c in range(2):
        rows, seen = slice(c * step, (c + 1) * step), slice(0, (c + 1) * step)
        row_id = lax.broadcasted_iota(jnp.int32, (step, (c + 1) * step), 0) + c * step
        key_id = lax.broadcasted_iota(jnp.int32, (step, (c + 1) * step), 1)
        visible = (seg_col[rows, :] == seg_row[:, seen]) & (row_id >= key_id)
        for g in range(k.shape[1] // HEAD_DIM):
            keys, values = head(k, seen, g), head(v, seen, g)
            for h in range(g * groups, (g + 1) * groups):
                s = dot(head(q, rows, h), keys, NT) * HEAD_DIM**-0.5
                s = jnp.where(visible, s, NEGATIVE)
                peak = jnp.max(s, axis=1, keepdims=True)
                e = jnp.exp(s - peak)
                total = jnp.sum(e, axis=1, keepdims=True)
                p = (e * (1.0 / total)).astype(BF16)
                o[rows, h * HEAD_DIM : (h + 1) * HEAD_DIM] = dot(p, values).astype(BF16)
                stat[rows, h : h + 1] = peak + jnp.log(total)
    sums[...] = jnp.transpose(stat[...])[: sums.shape[0]]
    part[...] = dot(o[...], wo[...]).astype(BF16)


def attend(x, gain, wq, wk, wv, wo, cosine, sine, seg_col, seg_row):
    tokens, model = x.shape
    out = jax.ShapeDtypeStruct
    heads = wq.shape[1] // HEAD_DIM
    return pl.pallas_call(
        attend_kernel,
        out_shape=[
            out((tokens, model), BF16),
            out((tokens, wq.shape[1]), BF16),
            out((tokens, wk.shape[1]), BF16),
            out((tokens, wv.shape[1]), BF16),
            out((tokens, wq.shape[1]), BF16),
            out((-(-heads // 8) * 8, tokens), F32),
            out((tokens, model), BF16),
        ],
        scratch_shapes=[pltpu.VMEM((tokens, 128), F32)],
        compiler_params=pltpu.CompilerParams(vmem_limit_bytes=VMEM_LIMIT),
        cost_estimate=SMALL,
        name="attend",
    )(x, gain, wq, wk, wv, wo, cosine, sine, seg_col, seg_row)


def attend_back_kernel(
    dh, wq, wk, wv, wo, cosine, sine, seg_col, seg_row, normed, q, k, v, sums,
    weights, back, dout, dq, dk, dv, low,
):
    tokens = dh.shape[0]
    groups = HEADS // KV_HEADS
    scale = HEAD_DIM**-0.5
    dout[...] = dot(dh[...], wo[...], NT).astype(BF16)
    dk[...] = jnp.zeros_like(dk)
    dv[...] = jnp.zeros_like(dv)
    step = tokens // 2
    for c in range(2):
        rows, seen = slice(c * step, (c + 1) * step), slice(0, (c + 1) * step)
        key_id = lax.broadcasted_iota(jnp.int32, ((c + 1) * step, step), 0)
        row_id = lax.broadcasted_iota(jnp.int32, ((c + 1) * step, step), 1) + c * step
        visible = (seg_col[seen, :] == seg_row[:, rows]) & (row_id >= key_id)
        for g in range(k.shape[1] // HEAD_DIM):
            keys, values = head(k, seen, g), head(v, seen, g)
            key_sum = value_sum = None
            for h in range(g * groups, (g + 1) * groups):
                query, grad = head(q, rows, h), head(dout, rows, h)
                s = jnp.where(visible, dot(keys, query, NT) * scale, NEGATIVE)
                p = jnp.exp(s - sums[h : h + 1, rows])
                dp = dot(values, grad, NT)
                balance = jnp.sum(p * dp, axis=0, keepdims=True)
                ds = (p * (dp - balance) * scale).astype(BF16)
                dq[rows, h * HEAD_DIM : (h + 1) * HEAD_DIM] = dot(ds, keys, TN)
                own = dot(ds, query)
                key_sum = own if key_sum is None else key_sum + own
                own = dot(p.astype(BF16), grad)
                value_sum = own if value_sum is None else value_sum + own
            dk[seen, g * HEAD_DIM : (g + 1) * HEAD_DIM] += key_sum
            dv[seen, g * HEAD_DIM : (g + 1) * HEAD_DIM] += value_sum
    at = 0
    for ref in (dq, dk):
        for piece in spin(ref[...], cosine[...], -sine[...]):
            low[:, at : at + 128] = piece.astype(BF16)
            at += 128
    low[:, at:] = dv[...].astype(BF16)
    one, two = wq.shape[1], wq.shape[1] + wk.shape[1]
    total = dot(low[:, :one], wq[...], NT) + dot(low[:, one:two], wk[...], NT)
    back[...] = (total + dot(low[:, two:], wv[...], NT)).astype(BF16)
    weights[...] = dot(normed[...], low[...], TN).astype(BF16)


def attend_back(dh, wq, wk, wv, wo, cosine, sine, seg_col, seg_row, normed, q, k, v, sums):
    tokens, model = dh.shape
    out = jax.ShapeDtypeStruct
    columns = wq.shape[1] + wk.shape[1] + wv.shape[1]
    return pl.pallas_call(
        attend_back_kernel,
        out_shape=[out((model, columns), BF16), out((tokens, model), BF16)],
        scratch_shapes=[
            pltpu.VMEM((tokens, wq.shape[1]), BF16),
            pltpu.VMEM((tokens, wq.shape[1]), F32),
            pltpu.VMEM((tokens, wk.shape[1]), F32),
            pltpu.VMEM((tokens, wk.shape[1]), F32),
            pltpu.VMEM((tokens, columns), BF16),
        ],
        compiler_params=pltpu.CompilerParams(vmem_limit_bytes=VMEM_LIMIT),
        cost_estimate=SMALL,
        name="attend_back",
    )(dh, wq, wk, wv, wo, cosine, sine, seg_col, seg_row, normed, q, k, v, sums)


class Places:
    def __init__(self):
        self.count = lax.axis_size("dp")
        self.ring = self.count // 4
        me = lax.axis_index("dp")
        self.z, self.y, self.x = me // 4, (me // 2) % 2, me % 2
        self.t = lax.axis_index("tensor")
        self.sent = {"x": [], "y": [], "z": []}
        self.after = self.single = None

    def send(self, axis, array, pairs):
        sent = self.sent[axis]
        first = sent[-1:] if axis == self.single else sent[-2:-1]
        if self.after is not None:
            first.append(self.after)
        if first:
            array = lax.optimization_barrier((array, *first))[0]
        got = lax.ppermute(array, "dp", pairs)
        sent.append(got)
        return got

    def by_x(self, array):
        return self.send("x", array, [(i, i ^ 1) for i in range(self.count)])

    def by_y(self, array):
        return self.send("y", array, [(i, i ^ 2) for i in range(self.count)])

    def by_z(self, array, step=1):
        return self.send(
            "z", array, [(i, (i + 4 * step) % self.count) for i in range(self.count)]
        )

    def by_ring(self, array, step):
        return lax.ppermute(
            array, "dp", [(i, (i + 4 * step) % self.count) for i in range(self.count)]
        )

    def by_t(self, array):
        return lax.ppermute(array, "tensor", [(0, 1), (1, 0)])

    def by(self, axis, array):
        return self.by_x(array) if axis == "x" else self.by_y(array)

    def spread_near(self, block):
        return block, self.by_x(block), self.by_y(block)

    def spread_far(self, own, beside_x, beside_y):
        half = own.shape[0] // 2
        return (
            own, beside_x, beside_y, self.by_y(beside_x[:half]), self.by_x(beside_y[half:])
        )

    def collect_far(self, near, far, order):
        return add(near, self.by(order[1], far))

    def collect_near(self, near, order):
        half = near.shape[0] // 2
        return add(near[:half], self.by(order[0], near[half:]))

    def number(self, j, label):
        y, x, half = label
        device = ((self.z - j) % self.ring) * 4 + (self.y ^ y) * 2 + (self.x ^ x)
        return device * 2 + half

    def sum_all(self, array):
        rows, columns = array.shape
        part = rows // self.count
        grid = array.reshape(self.ring, 2, 2, part, columns)
        half = columns // 2

        def split(value, place, axis):
            keep = lax.dynamic_index_in_dim(value, place, axis, keepdims=False)
            send = lax.dynamic_index_in_dim(value, 1 - place, axis, keepdims=False)
            return keep, send

        def join(own, other, place, axis):
            return jnp.where(
                place == 0, jnp.stack([own, other], axis), jnp.stack([other, own], axis)
            )

        keep_one, one = split(grid[..., :half], self.x, 2)
        keep_two, two = split(grid[..., half:], self.y, 1)
        one, two = add(keep_one, self.by_x(one)), add(keep_two, self.by_y(two))
        yield one
        keep_one, one = split(one, self.y, 1)
        keep_two, two = split(two, self.x, 1)
        one, two = add(keep_one, self.by_y(one)), add(keep_two, self.by_x(two))
        both = jnp.concatenate([one, two], axis=-1)
        yield

        def at(j):
            return lax.dynamic_index_in_dim(both, (self.z - j) % self.ring, 0, keepdims=False)

        got = [self.by_ring(at(j), -j) for j in range(1, self.ring)]
        total = sum((value.astype(F32) for value in got), at(0).astype(F32)).astype(BF16)
        got = [total]
        for j in range(1, self.ring):
            got.append(self.by_ring(total, j))
        got = jnp.stack(got)
        got = jnp.stack(
            [
                lax.dynamic_index_in_dim(got, (self.z - i) % self.ring, 0, keepdims=False)
                for i in range(self.ring)
            ]
        )
        one, two = got[..., :half], got[..., half:]
        yield
        other_one, other_two = self.by_y(one), self.by_x(two)
        one, two = join(one, other_one, self.y, 1), join(two, other_two, self.x, 1)
        yield
        other_one, other_two = self.by_x(one), self.by_y(two)
        one, two = join(one, other_one, self.x, 2), join(two, other_two, self.y, 1)
        yield jnp.concatenate([one, two], axis=-1).reshape(rows, columns)

    def own_half(self, array):
        half = array.shape[0] // 2
        return lax.dynamic_slice_in_dim(array, self.t * half, half, 0)

    def other_half(self, array):
        half = array.shape[0] // 2
        return lax.dynamic_slice_in_dim(array, (1 - self.t) * half, half, 0)

    def sum_halves(self, array):
        return self.own_half(array).astype(F32) + self.by_t(self.other_half(array)).astype(F32)

    def both_halves(self, array):
        other = self.by_t(array)
        return jnp.where(
            self.t == 0,
            jnp.concatenate([array, other], axis=0),
            jnp.concatenate([other, array], axis=0),
        )


def add(left, right):
    return (left.astype(F32) + right.astype(F32)).astype(left.dtype)


def frequencies():
    index = jnp.arange(128) % (HEAD_DIM // 2)
    return jnp.exp(index.astype(F32) * (-2.0 * math.log(10000.0) / HEAD_DIM))


def norm_back(values, inverse, gain, grad):
    scaled = gain * grad
    mean = jnp.mean(scaled * values, axis=-1, keepdims=True)
    return inverse * scaled - values * (inverse * inverse * inverse * mean)


def inverse_rms(values):
    return lax.rsqrt(jnp.mean(values * values, axis=-1, keepdims=True) + EPSILON)


def on_device(
    layer_input,
    doc_lengths,
    routes,
    norm1_gain,
    w_query,
    w_key,
    w_value,
    w_out,
    norm2_gain,
    w_router,
    w_gate,
    w_up,
    w_down,
    cotangent,
):
    places = Places()
    ring, count = places.ring, places.count
    tokens, model = layer_input.shape
    half = tokens // 2
    quarter = half // 2
    experts = w_router.shape[1]
    splits = count // experts
    gain_one = norm1_gain.astype(F32)
    gain_two = norm2_gain.astype(F32)

    dy = places.own_half(cotangent)
    block = places.spread_near(dy)
    ring_piece = dy[quarter:]
    pieces = [places.by_z(ring_piece)]
    block = places.spread_far(*block)
    wide = jnp.concatenate([piece[:quarter] for piece in block[:4]], axis=0)
    dy_second = [tuple(block[i][quarter:] for i in range(3)) + (block[4],)]
    for j in range(1, ring):
        if j + 1 < ring:
            pieces.append(places.by_z(pieces[-1]))
        beside = places.by_x(pieces[j - 1]), places.by_y(pieces[j - 1])
        far = places.by_y(beside[0]) if j % 2 else places.by_x(beside[1])
        dy_second.append((pieces[j - 1], *beside, far))
    dy_first = [wide, places.by_z(wide)]

    wg = lax.all_gather(w_gate[0], "tensor")
    wu = lax.all_gather(w_up[0], "tensor")
    wd = lax.all_gather(w_down[0], "tensor")

    named = jnp.any(
        places.own_half(routes)[:, :, None] == jnp.arange(experts, dtype=jnp.int32), axis=1
    )
    bits = jnp.sum(
        jnp.where(named, jnp.left_shift(1, jnp.arange(experts, dtype=jnp.int32)), 0), axis=1
    )
    bits = lax.all_to_all(
        jnp.broadcast_to(bits[None], (count, half)), "dp", split_axis=0, concat_axis=0, tiled=True
    ).reshape(2 * count, quarter)

    lengths = doc_lengths[0]
    index = jnp.arange(tokens, dtype=jnp.int32)
    ends = jnp.cumsum(lengths)
    starts = ends - lengths
    segment = jnp.sum((index[:, None] >= ends[None, :]).astype(jnp.int32), axis=1)
    slots = jnp.arange(lengths.shape[0], dtype=jnp.int32)
    first = jnp.sum(jnp.where(segment[:, None] == slots[None, :], starts[None, :], 0), axis=1)
    angles = (index - first).astype(F32)[:, None] * frequencies()[None, :]
    cosine = jnp.cos(angles)
    sine = jnp.sin(angles) * jnp.where(jnp.arange(128) % HEAD_DIM < HEAD_DIM // 2, -1.0, 1.0)
    around = (cosine, sine, segment[:, None], segment[None, :])
    normed, queries, keys, values, mixed_heads, sums, part = attend(
        layer_input, norm1_gain[None], w_query, w_key, w_value, w_out, *around
    )
    part, bits = lax.optimization_barrier((part, bits))
    attention = places.sum_halves(part)
    inputs_half = places.own_half(layer_input).astype(F32)
    hidden = inputs_half + attention
    inverse_two = inverse_rms(hidden)
    normed_two = (hidden * inverse_two * gain_two).astype(BF16)

    router_rows = w_router.T
    expert = lax.axis_index("dp") // splits
    gate_grads = jnp.zeros((2 * count, quarter), F32)

    tables = (SPREAD, SPLIT, near_far("xy", 0) + near_far("yx", 1))
    dy_blocks, results, kept = [], [], []

    def run(j):
        numbers = jnp.stack([places.number(j, label) for label in LABELS] + [expert])
        dy_blocks.append((dy_first[j], *dy_second[j]))
        mix, seed = results[-1][1:3] if results else (None, gate_grads)
        results.append(
            routed(
                numbers.astype(jnp.int32), bits, hn_blocks[j], dy_blocks[j], mix, seed, router_rows,
                wg, wu, wd, tables,
            )
        )
        places.after = results[-1][2]
        kept.append(results[-1][3:5])

    def near(j):
        hn_blocks[j] = places.spread_near(ring_blocks[j])

    def far(j):
        hn_blocks[j] = places.spread_far(*hn_blocks[j])

    def back_far(j):
        parts = results[j][0]
        back[j] = [
            places.collect_far(*parts[0:2], "xy"), places.collect_far(*parts[2:4], "yx")
        ]

    def back_near(j):
        parts = [places.collect_near(part, order) for part, order in zip(back[j], ("xy", "yx"))]
        back[j] = jnp.concatenate(parts, axis=0)

    def back_ring(j):
        back[j] = places.by_z(back[j], -j)

    def onward(running, value):
        return value if running is None else add(places.by_z(running), value)

    def grads_of(blocks, before):
        per = 4
        for at in range(0, len(blocks), per):
            span = blocks[at : at + per]
            before = expert_grads(
                [hn_blocks[i] for i in span],
                [dy_blocks[i] for i in span],
                [kept[i][0] for i in span],
                [kept[i][1] for i in span],
                [tables[:2] for i in span],
                before,
            )
        return before

    ring_blocks = [normed_two, places.by_z(normed_two)]
    hn_blocks, back = [None] * ring, [None] * ring
    near(0)
    near(1)
    far(0)
    for j in range(ring):
        if j + 2 < ring:
            ring_blocks.append(places.by_z(ring_blocks[-1]))
            dy_first.append(places.by_z(dy_first[-1]))
            near(j + 2)
        if j + 1 < ring:
            far(j + 1)
        if j > 2:
            places.single = "z"
            back_near(j - 2)
            back_ring(j - 2)
        if j > 1:
            back_far(j - 1)
        run(j)
    last = ring - 1
    back_far(last)
    if last > 1:
        back_near(last - 1)
        back_ring(last - 1)
    places.after = None
    kept = lax.optimization_barrier((kept, results[last][2]))[0]
    expert_sums = grads_of(range(ring), ())
    places.after = expert_sums[1]
    back_near(last)
    back_far(0)
    places.after = back[0]
    back_ring(last)
    places.after = None
    back_near(0)
    mixture = lax.optimization_barrier((results[-1][1], back[last]))[0]
    normed_grad = sum(part.astype(F32) for part in back)
    gate_grads = lax.all_to_all(
        results[-1][2].reshape(count, half), "dp", split_axis=0, concat_axis=0, tiled=True
    )
    gate_grads = jnp.sum(gate_grads.reshape(experts, splits, half), axis=1).T

    logits = jnp.where(named, dot(normed_two, w_router), NEGATIVE)
    gates = jax.nn.softmax(logits, axis=-1)
    logit_grad = gates * (gate_grads - jnp.sum(gates * gate_grads, axis=-1, keepdims=True))
    logit_grad = logit_grad.astype(BF16)
    grad_router = dot(logit_grad, normed_two, TN)
    normed_grad = normed_grad + dot(logit_grad, w_router, NT)
    grad_gain_two = jnp.sum(normed_grad * hidden * inverse_two, axis=0)
    hidden_grad = dy.astype(F32) + norm_back(hidden, inverse_two, gain_two, normed_grad)
    hidden_low = places.both_halves(hidden_grad.astype(BF16))
    mixture = lax.psum_scatter(mixture, "dp", scatter_dimension=0, tiled=True)
    mixture = mixture.astype(F32)
    grad_out = dot(mixed_heads, hidden_low, TN).astype(BF16)

    grad_heads_w, part = attend_back(
        hidden_low, w_query, w_key, w_value, w_out, *around, normed, queries, keys, values, sums
    )
    grad_heads_w = places.sum_all(grad_heads_w)
    begun = next(grad_heads_w)
    normed_grad_one = places.sum_halves(part)
    inverse_half = inverse_rms(inputs_half)
    grad_gain_one = jnp.sum(normed_grad_one * inputs_half * inverse_half, axis=0)
    grad_input = hidden_grad + norm_back(inputs_half, inverse_half, gain_one, normed_grad_one)
    grad_input = places.both_halves(grad_input.astype(BF16))

    small = jnp.concatenate([grad_router, grad_gain_one[None], grad_gain_two[None]], axis=0)
    small = (small + places.by_t(small)).astype(BF16)
    rows, columns = grad_out.shape
    spare = 256 * (-(-small.size // (256 * rows)))
    small = jnp.pad(small.reshape(-1), (0, rows * spare - small.size)).reshape(rows, spare)
    grad_out = places.sum_all(jnp.concatenate([grad_out, small], axis=1))
    next(grad_out)
    next(grad_heads_w)
    next(grad_out)
    next(grad_heads_w)
    next(grad_out)
    next(grad_heads_w)
    next(grad_out)
    grad_heads_w = next(grad_heads_w).astype(F32)
    grad_out = next(grad_out).astype(F32)
    small = grad_out[:, columns:].reshape(-1)[: (experts + 2) * model].reshape(-1, model)
    grad_out = grad_out[:, :columns]
    output = places.both_halves((hidden + mixture).astype(BF16))

    grad_gu = lax.psum_scatter(expert_sums[0], "tensor", scatter_dimension=0)
    grad_d = lax.psum_scatter(expert_sums[1], "tensor", scatter_dimension=0, tiled=True)
    width = w_gate.shape[2]
    query_width, key_width = w_query.shape[1], w_key.shape[1]
    return (
        output,
        grad_input,
        small[experts],
        grad_heads_w[:, :query_width],
        grad_heads_w[:, query_width : query_width + key_width],
        grad_heads_w[:, query_width + key_width :],
        grad_out,
        small[experts + 1],
        small[:experts].T,
        grad_gu[None, :, :width],
        grad_gu[None, :, width:],
        grad_d[None],
    )


def solution(mesh):
    in_specs = (
        P("dp", None),
        P("dp", None),
        P("dp", None),
        P(),
        P(None, "tensor"),
        P(None, "tensor"),
        P(None, "tensor"),
        P("tensor", None),
        P(),
        P(),
        P("dp", None, "tensor"),
        P("dp", None, "tensor"),
        P("dp", "tensor", None),
        P("dp", None),
    )
    out_specs = (
        P("dp", None),
        P("dp", None),
        P(),
        P(None, "tensor"),
        P(None, "tensor"),
        P(None, "tensor"),
        P("tensor", None),
        P(),
        P(),
        P("dp", None, "tensor"),
        P("dp", None, "tensor"),
        P("dp", "tensor", None),
    )
    return jax.shard_map(
        on_device, mesh=mesh, in_specs=in_specs, out_specs=out_specs, check_vma=False
    )
```

```python
import functools
import math

import jax
import jax.numpy as jnp
from jax import lax
from jax.experimental import pallas as pl
from jax.experimental.pallas import tpu as pltpu
from jax.sharding import PartitionSpec as P

HEAD_DIM = 64
HEADS = 24
KV_HEADS = 8
EPSILON = 1e-06
NEGATIVE = -1e30
BF16 = jnp.bfloat16
F32 = jnp.float32
NN = (((1,), (0,)), ((), ()))
NT = (((1,), (1,)), ((), ()))
TN = (((0,), (0,)), ((), ()))
VMEM_LIMIT = 56 * 1024 * 1024
SMALL = pl.CostEstimate(flops=0, bytes_accessed=1024 * 1024, transcendentals=0)


def dot(left, right, dims=NN):
    return lax.dot_general(left, right, dims, preferred_element_type=F32)


LABELS = [(0, 0, 0), (0, 0, 1), (0, 1, 0), (0, 1, 1), (1, 0, 0), (1, 0, 1), (1, 1, 0), (1, 1, 1)]
SPREAD = [
    [(0, 0, 0), (0, 0, 1)],
    [(0, 1, 0), (0, 1, 1)],
    [(1, 0, 0), (1, 0, 1)],
    [(1, 1, 0)],
    [(1, 1, 1)],
]
WIDE = [(0, 0, 0), (0, 1, 0), (1, 0, 0), (1, 1, 0)]
SPLIT = [WIDE, [(0, 0, 1)], [(0, 1, 1)], [(1, 0, 1)], [(1, 1, 1)]]


def near_far(order, half):
    if order == "xy":
        return [[(0, 0, half), (0, 1, half)], [(1, 0, half), (1, 1, half)]]
    return [[(0, 0, half), (1, 0, half)], [(0, 1, half), (1, 1, half)]]


def places_of(tables):
    return {label: (a, i) for a, table in enumerate(tables) for i, label in enumerate(table)}


def piece_of(refs, where, label, rows):
    array, at = where[label]
    return refs[array].at[pl.ds(at * rows, rows)]


def routed_kernel(tables, fresh, *refs):
    counts = [len(table) for table in tables]
    groups, at = [], 2
    for size in (counts[0], counts[1], 1, 1, 1, 1, 1, 0 if fresh else 1, counts[2], 1, 1, 1, 1, 6):
        groups.append(refs[at : at + size])
        at += size
    numbers, bits = refs[0], refs[1]
    hn, dy, (seed,), (router,), (wg,), (wu,), (wd,), _, dx, (mix,), *rest = groups
    (dgate,), (pre,), (act,), scratch = rest
    hbuf, dbuf, xbuf, mbuf, in_sem, out_sem = scratch
    where = [places_of(table) for table in tables]
    rows = hbuf.shape[1] // 2
    step = pl.program_id(0)
    slot = lax.rem(step, 2)

    def fetch(s, to):
        return [
            pltpu.make_async_copy(
                piece_of(source, where[n], LABELS[2 * s + i], rows),
                buffer.at[to, pl.ds(i * rows, rows)],
                in_sem.at[to, 2 * n + i],
            )
            for n, (source, buffer) in enumerate(((hn, hbuf), (dy, dbuf)))
            for i in range(2)
        ]

    def put(s, at):
        copies = []
        for i in range(2):
            p, span = 2 * s + i, pl.ds(i * rows, rows)
            target = piece_of(dx, where[2], LABELS[p], rows)
            copies.append(
                pltpu.make_async_copy(xbuf.at[at, span], target, out_sem.at[at, i])
            )
            target = mix.at[pl.ds(pl.multiple_of(numbers[p] * rows, rows), rows)]
            copies.append(
                pltpu.make_async_copy(mbuf.at[at, span], target, out_sem.at[at, 2 + i])
            )
        return copies

    @pl.when(step == 0)
    def _():
        for copy in fetch(0, 0):
            copy.start()
        dgate[...] = seed[...]

    for s in range(1, 4):

        @pl.when(step == s - 1)
        def _():
            for copy in fetch(s, s % 2):
                copy.start()

    for copy in fetch(0, slot):
        copy.wait()
    for s in range(2, 4):

        @pl.when(step == s)
        def _():
            for copy in put(s - 2, s % 2):
                copy.wait()

    tokens = hbuf[slot]
    grads = dbuf[slot]
    experts = router.shape[0]
    columns = jnp.transpose(bits[...])
    lane = lax.broadcasted_iota(jnp.int32, columns.shape, 1)
    ids = [numbers[2 * step], numbers[2 * step + 1]]
    flags = jnp.concatenate(
        [jnp.sum(jnp.where(lane == i, columns, 0), axis=1, keepdims=True) for i in ids], axis=0
    )
    lane = lax.broadcasted_iota(jnp.int32, (2 * rows, experts), 1)
    named = jnp.bitwise_and(lax.shift_right_logical(flags + jnp.zeros_like(lane), lane), 1) == 1
    logits = jnp.where(named, dot(tokens, router[...], NT), NEGATIVE)
    weights = jnp.exp(logits - jnp.max(logits, axis=1, keepdims=True))
    gate = jnp.sum(jnp.where(lane == numbers[8], weights, 0.0), axis=1, keepdims=True)
    gate = gate / jnp.sum(weights, axis=1, keepdims=True)
    width = wg.shape[2]
    back = mixed = gate_grad = None
    for c in range(2):
        gu = dot(tokens, wg[c])
        up = dot(tokens, wu[c])
        da = dot(grads, wd[c], NT)
        sig = 1.0 / (1.0 + jnp.exp(-gu))
        silu = gu * sig
        value = silu * up
        own = jnp.sum(value * da, axis=1, keepdims=True)
        gate_grad = own if c == 0 else gate_grad + own
        low = (value * gate).astype(BF16)
        act[:, c * width : (c + 1) * width] = low
        own = dot(low, wd[c])
        mixed = own if c == 0 else mixed + own
        da = da * gate
        dgu = (da * up * sig * (1.0 + gu * (1.0 - sig))).astype(BF16)
        dup = (da * silu).astype(BF16)
        pre[:, 2 * c * width : (2 * c + 1) * width] = dgu
        pre[:, (2 * c + 1) * width : (2 * c + 2) * width] = dup
        own = dot(dgu, wg[c], NT) + dot(dup, wu[c], NT)
        back = own if c == 0 else back + own
    xbuf[slot] = back.astype(BF16)
    mbuf[slot] = mixed.astype(BF16)
    for i in range(2):
        piece = jnp.broadcast_to(gate_grad[i * rows : (i + 1) * rows], (rows, rows))
        dgate[pl.ds(ids[i], 1), :] = jnp.transpose(piece)[:1]
    for s in range(4):

        @pl.when(step == s)
        def _():
            for copy in put(s, s % 2):
                copy.start()

    @pl.when(step == 3)
    def _():
        for copy in put(2, 0) + put(3, 1):
            copy.wait()


def routed(numbers, bits, hn, dy, mix, seed, router, wg, wu, wd, tables):
    model = hn[0].shape[1]
    rows = bits.shape[1]
    width = wg.shape[2]
    hbm = pl.BlockSpec(memory_space=pl.ANY)

    def full(array):
        return pl.BlockSpec(array.shape, lambda i: (0,) * array.ndim)

    def tile(columns):
        return pl.BlockSpec((2 * rows, columns), lambda i: (i, 0))

    out = jax.ShapeDtypeStruct
    outs = [out((len(table) * rows, model), BF16) for table in tables[2]]
    outs.append(out((bits.shape[0] * rows, model), BF16))
    mix = [] if mix is None else [mix]
    before = 2 + len(hn) + len(dy)
    got = pl.pallas_call(
        functools.partial(routed_kernel, tables, not mix),
        grid=(4,),
        in_specs=[pl.BlockSpec(memory_space=pltpu.SMEM), full(bits)]
        + [hbm] * (len(hn) + len(dy))
        + [full(array) for array in (seed, router, wg, wu, wd)]
        + [hbm] * len(mix),
        out_specs=[hbm] * len(outs) + [full(seed), tile(4 * width), tile(2 * width)],
        out_shape=outs
        + [
            out(seed.shape, F32),
            out((8 * rows, 4 * width), BF16),
            out((8 * rows, 2 * width), BF16),
        ],
        scratch_shapes=[pltpu.VMEM((2, 2 * rows, model), BF16)] * 4
        + [pltpu.SemaphoreType.DMA((2, 4))] * 2,
        input_output_aliases={before: len(outs)}
        | ({before + 5: len(outs) - 1} if mix else {}),
        compiler_params=pltpu.CompilerParams(vmem_limit_bytes=VMEM_LIMIT),
        cost_estimate=SMALL,
        name="routed_rows",
    )(numbers, bits, *hn, *dy, seed, router, wg, wu, wd, *mix)
    split = len(tables[2])
    return got[:split], *got[split:]


def expert_grads_kernel(tables, fresh, *refs):
    blocks = len(tables)
    at, hn, dy = 0, [], []
    for into, n in ((hn, 0), (dy, 1)):
        for table in tables:
            into.append(refs[at : at + len(table[n])])
            at += len(table[n])
    pre, act = refs[at : at + blocks], refs[at + blocks : at + 2 * blocks]
    at += 2 * blocks
    if not fresh:
        gu_before, gd_before = refs[at : at + 2]
        at += 2
    gu, gd, hbuf, dbuf, pbuf, abuf, sem = refs[at:]
    step = pl.program_id(0)
    slot = lax.rem(step, 2)
    rows = hbuf.shape[1] // 2

    def fetch(s, to):
        j, s = s // 4, s % 4
        copies = [
            pltpu.make_async_copy(
                piece_of(source[j], places_of(tables[j][n]), LABELS[2 * s + i], rows),
                buffer.at[to, pl.ds(i * rows, rows)],
                sem.at[to, 2 * n + i],
            )
            for n, (source, buffer) in enumerate(((hn, hbuf), (dy, dbuf)))
            for i in range(2)
        ]
        span = pl.ds(2 * s * rows, 2 * rows)
        return copies + [
            pltpu.make_async_copy(pre[j].at[span], pbuf.at[to], sem.at[to, 4]),
            pltpu.make_async_copy(act[j].at[span], abuf.at[to], sem.at[to, 5]),
        ]

    @pl.when(step == 0)
    def _():
        for copy in fetch(0, 0):
            copy.start()
        gu[...] = jnp.zeros_like(gu) if fresh else gu_before[...]
        gd[...] = jnp.zeros_like(gd) if fresh else gd_before[...]

    for s in range(1, 4 * blocks):

        @pl.when(step == s - 1)
        def _():
            for copy in fetch(s, s % 2):
                copy.start()

    for copy in fetch(0, slot):
        copy.wait()
    width = gu.shape[2]
    for c in range(2):
        gu[c] += dot(hbuf[slot], pbuf[slot, :, c * width : (c + 1) * width], TN)
    gd[...] += dot(abuf[slot], dbuf[slot], TN)


def expert_grads(hn, dy, pre, act, tables, before):
    blocks = len(pre)
    rows, model = pre[0].shape[0] // 8, hn[0][0].shape[1]
    four, two = pre[0].shape[1], act[0].shape[1]
    hbm = pl.BlockSpec(memory_space=pl.ANY)
    out = jax.ShapeDtypeStruct
    flat = [array for group in (*hn, *dy) for array in group]
    sums = [
        pl.BlockSpec((2, model, two), lambda i: (0, 0, 0)),
        pl.BlockSpec((two, model), lambda i: (0, 0)),
    ]
    fixed = len(flat) + 2 * blocks
    return pl.pallas_call(
        functools.partial(expert_grads_kernel, tables, not before),
        grid=(4 * blocks,),
        in_specs=[hbm] * fixed + (sums if before else []),
        out_specs=sums,
        out_shape=[out((2, model, two), F32), out((two, model), F32)],
        scratch_shapes=[
            pltpu.VMEM((2, 2 * rows, model), BF16),
            pltpu.VMEM((2, 2 * rows, model), BF16),
            pltpu.VMEM((2, 2 * rows, four), BF16),
            pltpu.VMEM((2, 2 * rows, two), BF16),
            pltpu.SemaphoreType.DMA((2, 6)),
        ],
        input_output_aliases={fixed: 0, fixed + 1: 1} if before else {},
        compiler_params=pltpu.CompilerParams(vmem_limit_bytes=VMEM_LIMIT),
        cost_estimate=SMALL,
        name="expert_grads",
    )(*flat, *pre, *act, *before)


def spin(values, cosine, sine):
    lane = lax.broadcasted_iota(jnp.int32, cosine.shape, 1) % HEAD_DIM
    parts = []
    for at in range(0, values.shape[1], 128):
        part = values[:, at : at + 128]
        other = jnp.where(
            lane < HEAD_DIM // 2,
            pltpu.roll(part, 128 - HEAD_DIM // 2, 1),
            pltpu.roll(part, HEAD_DIM // 2, 1),
        )
        parts.append(part * cosine + other * sine)
    return parts


def head(ref, rows, h):
    return ref[rows, h * HEAD_DIM : (h + 1) * HEAD_DIM]


def attend_kernel(
    x, gain, wq, wk, wv, wo, cosine, sine, seg_col, seg_row, normed, q, k, v, o, sums, part, stat
):
    tokens = x.shape[0]
    groups = HEADS // KV_HEADS
    inputs = x[...].astype(F32)
    inverse = lax.rsqrt(jnp.mean(inputs * inputs, axis=1, keepdims=True) + EPSILON)
    low = (inputs * inverse * gain[...].astype(F32)).astype(BF16)
    normed[...] = low
    for ref, weight in ((q, wq), (k, wk)):
        for i, piece in enumerate(spin(dot(low, weight[...]), cosine[...], sine[...])):
            ref[:, i * 128 : (i + 1) * 128] = piece.astype(BF16)
    v[...] = dot(low, wv[...]).astype(BF16)
    stat[...] = jnp.zeros_like(stat)
    step = tokens // 2
    for c in range(2):
        rows, seen = slice(c * step, (c + 1) * step), slice(0, (c + 1) * step)
        row_id = lax.broadcasted_iota(jnp.int32, (step, (c + 1) * step), 0) + c * step
        key_id = lax.broadcasted_iota(jnp.int32, (step, (c + 1) * step), 1)
        visible = (seg_col[rows, :] == seg_row[:, seen]) & (row_id >= key_id)
        for g in range(k.shape[1] // HEAD_DIM):
            keys, values = head(k, seen, g), head(v, seen, g)
            for h in range(g * groups, (g + 1) * groups):
                s = dot(head(q, rows, h), keys, NT) * HEAD_DIM**-0.5
                s = jnp.where(visible, s, NEGATIVE)
                peak = jnp.max(s, axis=1, keepdims=True)
                e = jnp.exp(s - peak)
                total = jnp.sum(e, axis=1, keepdims=True)
                p = (e * (1.0 / total)).astype(BF16)
                o[rows, h * HEAD_DIM : (h + 1) * HEAD_DIM] = dot(p, values).astype(BF16)
                stat[rows, h : h + 1] = peak + jnp.log(total)
    sums[...] = jnp.transpose(stat[...])[: sums.shape[0]]
    part[...] = dot(o[...], wo[...]).astype(BF16)


def attend(x, gain, wq, wk, wv, wo, cosine, sine, seg_col, seg_row):
    tokens, model = x.shape
    out = jax.ShapeDtypeStruct
    heads = wq.shape[1] // HEAD_DIM
    return pl.pallas_call(
        attend_kernel,
        out_shape=[
            out((tokens, model), BF16),
            out((tokens, wq.shape[1]), BF16),
            out((tokens, wk.shape[1]), BF16),
            out((tokens, wv.shape[1]), BF16),
            out((tokens, wq.shape[1]), BF16),
            out((-(-heads // 8) * 8, tokens), F32),
            out((tokens, model), BF16),
        ],
        scratch_shapes=[pltpu.VMEM((tokens, 128), F32)],
        compiler_params=pltpu.CompilerParams(vmem_limit_bytes=VMEM_LIMIT),
        cost_estimate=SMALL,
        name="attend",
    )(x, gain, wq, wk, wv, wo, cosine, sine, seg_col, seg_row)


def attend_back_kernel(
    dh, wq, wk, wv, wo, cosine, sine, seg_col, seg_row, normed, q, k, v, sums,
    weights, back, dout, dq, dk, dv, low,
):
    tokens = dh.shape[0]
    groups = HEADS // KV_HEADS
    scale = HEAD_DIM**-0.5
    dout[...] = dot(dh[...], wo[...], NT).astype(BF16)
    dk[...] = jnp.zeros_like(dk)
    dv[...] = jnp.zeros_like(dv)
    step = tokens // 2
    for c in range(2):
        rows, seen = slice(c * step, (c + 1) * step), slice(0, (c + 1) * step)
        key_id = lax.broadcasted_iota(jnp.int32, ((c + 1) * step, step), 0)
        row_id = lax.broadcasted_iota(jnp.int32, ((c + 1) * step, step), 1) + c * step
        visible = (seg_col[seen, :] == seg_row[:, rows]) & (row_id >= key_id)
        for g in range(k.shape[1] // HEAD_DIM):
            keys, values = head(k, seen, g), head(v, seen, g)
            key_sum = value_sum = None
            for h in range(g * groups, (g + 1) * groups):
                query, grad = head(q, rows, h), head(dout, rows, h)
                s = jnp.where(visible, dot(keys, query, NT) * scale, NEGATIVE)
                p = jnp.exp(s - sums[h : h + 1, rows])
                dp = dot(values, grad, NT)
                balance = jnp.sum(p * dp, axis=0, keepdims=True)
                ds = (p * (dp - balance) * scale).astype(BF16)
                dq[rows, h * HEAD_DIM : (h + 1) * HEAD_DIM] = dot(ds, keys, TN)
                own = dot(ds, query)
                key_sum = own if key_sum is None else key_sum + own
                own = dot(p.astype(BF16), grad)
                value_sum = own if value_sum is None else value_sum + own
            dk[seen, g * HEAD_DIM : (g + 1) * HEAD_DIM] += key_sum
            dv[seen, g * HEAD_DIM : (g + 1) * HEAD_DIM] += value_sum
    at = 0
    for ref in (dq, dk):
        for piece in spin(ref[...], cosine[...], -sine[...]):
            low[:, at : at + 128] = piece.astype(BF16)
            at += 128
    low[:, at:] = dv[...].astype(BF16)
    one, two = wq.shape[1], wq.shape[1] + wk.shape[1]
    total = dot(low[:, :one], wq[...], NT) + dot(low[:, one:two], wk[...], NT)
    back[...] = (total + dot(low[:, two:], wv[...], NT)).astype(BF16)
    weights[...] = dot(normed[...], low[...], TN).astype(BF16)


def attend_back(dh, wq, wk, wv, wo, cosine, sine, seg_col, seg_row, normed, q, k, v, sums):
    tokens, model = dh.shape
    out = jax.ShapeDtypeStruct
    columns = wq.shape[1] + wk.shape[1] + wv.shape[1]
    return pl.pallas_call(
        attend_back_kernel,
        out_shape=[out((model, columns), BF16), out((tokens, model), BF16)],
        scratch_shapes=[
            pltpu.VMEM((tokens, wq.shape[1]), BF16),
            pltpu.VMEM((tokens, wq.shape[1]), F32),
            pltpu.VMEM((tokens, wk.shape[1]), F32),
            pltpu.VMEM((tokens, wk.shape[1]), F32),
            pltpu.VMEM((tokens, columns), BF16),
        ],
        compiler_params=pltpu.CompilerParams(vmem_limit_bytes=VMEM_LIMIT),
        cost_estimate=SMALL,
        name="attend_back",
    )(dh, wq, wk, wv, wo, cosine, sine, seg_col, seg_row, normed, q, k, v, sums)


class Places:
    def __init__(self):
        self.count = lax.axis_size("dp")
        self.ring = self.count // 4
        me = lax.axis_index("dp")
        self.z, self.y, self.x = me // 4, (me // 2) % 2, me % 2
        self.t = lax.axis_index("tensor")
        self.sent = {"x": [], "y": [], "z": []}
        self.after = self.single = None

    def send(self, axis, array, pairs):
        sent = self.sent[axis]
        first = sent[-1:] if axis == self.single else sent[-2:-1]
        if self.after is not None:
            first.append(self.after)
        if first:
            array = lax.optimization_barrier((array, *first))[0]
        got = lax.ppermute(array, "dp", pairs)
        sent.append(got)
        return got

    def by_x(self, array):
        return self.send("x", array, [(i, i ^ 1) for i in range(self.count)])

    def by_y(self, array):
        return self.send("y", array, [(i, i ^ 2) for i in range(self.count)])

    def by_z(self, array, step=1):
        return self.send(
            "z", array, [(i, (i + 4 * step) % self.count) for i in range(self.count)]
        )

    def by_ring(self, array, step):
        return lax.ppermute(
            array, "dp", [(i, (i + 4 * step) % self.count) for i in range(self.count)]
        )

    def by_t(self, array):
        return lax.ppermute(array, "tensor", [(0, 1), (1, 0)])

    def by(self, axis, array):
        return self.by_x(array) if axis == "x" else self.by_y(array)

    def spread_near(self, block):
        return block, self.by_x(block), self.by_y(block)

    def spread_far(self, own, beside_x, beside_y):
        half = own.shape[0] // 2
        return (
            own, beside_x, beside_y, self.by_y(beside_x[:half]), self.by_x(beside_y[half:])
        )

    def collect_far(self, near, far, order):
        return add(near, self.by(order[1], far))

    def collect_near(self, near, order):
        half = near.shape[0] // 2
        return add(near[:half], self.by(order[0], near[half:]))

    def number(self, j, label):
        y, x, half = label
        device = ((self.z - j) % self.ring) * 4 + (self.y ^ y) * 2 + (self.x ^ x)
        return device * 2 + half

    def sum_all(self, array):
        rows, columns = array.shape
        part = rows // self.count
        grid = array.reshape(self.ring, 2, 2, part, columns)
        half = columns // 2

        def split(value, place, axis):
            keep = lax.dynamic_index_in_dim(value, place, axis, keepdims=False)
            send = lax.dynamic_index_in_dim(value, 1 - place, axis, keepdims=False)
            return keep, send

        def join(own, other, place, axis):
            return jnp.where(
                place == 0, jnp.stack([own, other], axis), jnp.stack([other, own], axis)
            )

        keep_one, one = split(grid[..., :half], self.x, 2)
        keep_two, two = split(grid[..., half:], self.y, 1)
        one, two = add(keep_one, self.by_x(one)), add(keep_two, self.by_y(two))
        yield one
        keep_one, one = split(one, self.y, 1)
        keep_two, two = split(two, self.x, 1)
        one, two = add(keep_one, self.by_y(one)), add(keep_two, self.by_x(two))
        both = jnp.concatenate([one, two], axis=-1)
        yield

        def at(j):
            return lax.dynamic_index_in_dim(both, (self.z - j) % self.ring, 0, keepdims=False)

        got = [self.by_ring(at(j), -j) for j in range(1, self.ring)]
        total = sum((value.astype(F32) for value in got), at(0).astype(F32)).astype(BF16)
        got = [total]
        for j in range(1, self.ring):
            got.append(self.by_ring(total, j))
        got = jnp.stack(got)
        got = jnp.stack(
            [
                lax.dynamic_index_in_dim(got, (self.z - i) % self.ring, 0, keepdims=False)
                for i in range(self.ring)
            ]
        )
        one, two = got[..., :half], got[..., half:]
        yield
        other_one, other_two = self.by_y(one), self.by_x(two)
        one, two = join(one, other_one, self.y, 1), join(two, other_two, self.x, 1)
        yield
        other_one, other_two = self.by_x(one), self.by_y(two)
        one, two = join(one, other_one, self.x, 2), join(two, other_two, self.y, 1)
        yield jnp.concatenate([one, two], axis=-1).reshape(rows, columns)

    def own_half(self, array):
        half = array.shape[0] // 2
        return lax.dynamic_slice_in_dim(array, self.t * half, half, 0)

    def other_half(self, array):
        half = array.shape[0] // 2
        return lax.dynamic_slice_in_dim(array, (1 - self.t) * half, half, 0)

    def sum_halves(self, array):
        return self.own_half(array).astype(F32) + self.by_t(self.other_half(array)).astype(F32)

    def both_halves(self, array):
        other = self.by_t(array)
        return jnp.where(
            self.t == 0,
            jnp.concatenate([array, other], axis=0),
            jnp.concatenate([other, array], axis=0),
        )


def add(left, right):
    return (left.astype(F32) + right.astype(F32)).astype(left.dtype)


def frequencies():
    index = jnp.arange(128) % (HEAD_DIM // 2)
    return jnp.exp(index.astype(F32) * (-2.0 * math.log(10000.0) / HEAD_DIM))


def norm_back(values, inverse, gain, grad):
    scaled = gain * grad
    mean = jnp.mean(scaled * values, axis=-1, keepdims=True)
    return inverse * scaled - values * (inverse * inverse * inverse * mean)


def inverse_rms(values):
    return lax.rsqrt(jnp.mean(values * values, axis=-1, keepdims=True) + EPSILON)


def on_device(
    layer_input,
    doc_lengths,
    routes,
    norm1_gain,
    w_query,
    w_key,
    w_value,
    w_out,
    norm2_gain,
    w_router,
    w_gate,
    w_up,
    w_down,
    cotangent,
):
    places = Places()
    ring, count = places.ring, places.count
    tokens, model = layer_input.shape
    half = tokens // 2
    quarter = half // 2
    experts = w_router.shape[1]
    splits = count // experts
    gain_one = norm1_gain.astype(F32)
    gain_two = norm2_gain.astype(F32)

    dy = places.own_half(cotangent)
    block = places.spread_near(dy)
    ring_piece = dy[quarter:]
    pieces = [places.by_z(ring_piece)]
    block = places.spread_far(*block)
    wide = jnp.concatenate([piece[:quarter] for piece in block[:4]], axis=0)
    dy_second = [tuple(block[i][quarter:] for i in range(3)) + (block[4],)]
    for j in range(1, ring):
        if j + 1 < ring:
            pieces.append(places.by_z(pieces[-1]))
        beside = places.by_x(pieces[j - 1]), places.by_y(pieces[j - 1])
        far = places.by_y(beside[0]) if j % 2 else places.by_x(beside[1])
        dy_second.append((pieces[j - 1], *beside, far))
    dy_first = [wide, places.by_z(wide)]

    wg = lax.all_gather(w_gate[0], "tensor")
    wu = lax.all_gather(w_up[0], "tensor")
    wd = lax.all_gather(w_down[0], "tensor")

    named = jnp.any(
        places.own_half(routes)[:, :, None] == jnp.arange(experts, dtype=jnp.int32), axis=1
    )
    bits = jnp.sum(
        jnp.where(named, jnp.left_shift(1, jnp.arange(experts, dtype=jnp.int32)), 0), axis=1
    )
    bits = lax.all_to_all(
        jnp.broadcast_to(bits[None], (count, half)), "dp", split_axis=0, concat_axis=0, tiled=True
    ).reshape(2 * count, quarter)

    lengths = doc_lengths[0]
    index = jnp.arange(tokens, dtype=jnp.int32)
    ends = jnp.cumsum(lengths)
    starts = ends - lengths
    segment = jnp.sum((index[:, None] >= ends[None, :]).astype(jnp.int32), axis=1)
    slots = jnp.arange(lengths.shape[0], dtype=jnp.int32)
    first = jnp.sum(jnp.where(segment[:, None] == slots[None, :], starts[None, :], 0), axis=1)
    angles = (index - first).astype(F32)[:, None] * frequencies()[None, :]
    cosine = jnp.cos(angles)
    sine = jnp.sin(angles) * jnp.where(jnp.arange(128) % HEAD_DIM < HEAD_DIM // 2, -1.0, 1.0)
    around = (cosine, sine, segment[:, None], segment[None, :])
    normed, queries, keys, values, mixed_heads, sums, part = attend(
        layer_input, norm1_gain[None], w_query, w_key, w_value, w_out, *around
    )
    part, bits = lax.optimization_barrier((part, bits))
    attention = places.sum_halves(part)
    inputs_half = places.own_half(layer_input).astype(F32)
    hidden = inputs_half + attention
    inverse_two = inverse_rms(hidden)
    normed_two = (hidden * inverse_two * gain_two).astype(BF16)

    router_rows = w_router.T
    expert = lax.axis_index("dp") // splits
    gate_grads = jnp.zeros((2 * count, quarter), F32)

    tables = (SPREAD, SPLIT, near_far("xy", 0) + near_far("yx", 1))
    dy_blocks, results, kept = [], [], []

    def run(j):
        numbers = jnp.stack([places.number(j, label) for label in LABELS] + [expert])
        dy_blocks.append((dy_first[j], *dy_second[j]))
        mix, seed = results[-1][1:3] if results else (None, gate_grads)
        results.append(
            routed(
                numbers.astype(jnp.int32), bits, hn_blocks[j], dy_blocks[j], mix, seed, router_rows,
                wg, wu, wd, tables,
            )
        )
        places.after = results[-1][2]
        kept.append(results[-1][3:5])

    def near(j):
        hn_blocks[j] = places.spread_near(ring_blocks[j])

    def far(j):
        hn_blocks[j] = places.spread_far(*hn_blocks[j])

    def back_far(j):
        parts = results[j][0]
        back[j] = [
            places.collect_far(*parts[0:2], "xy"), places.collect_far(*parts[2:4], "yx")
        ]

    def back_near(j):
        parts = [places.collect_near(part, order) for part, order in zip(back[j], ("xy", "yx"))]
        back[j] = jnp.concatenate(parts, axis=0)

    def back_ring(j):
        back[j] = places.by_z(back[j], -j)

    def onward(running, value):
        return value if running is None else add(places.by_z(running), value)

    def grads_of(blocks, before):
        per = 4
        for at in range(0, len(blocks), per):
            span = blocks[at : at + per]
            before = expert_grads(
                [hn_blocks[i] for i in span],
                [dy_blocks[i] for i in span],
                [kept[i][0] for i in span],
                [kept[i][1] for i in span],
                [tables[:2] for i in span],
                before,
            )
        return before

    ring_blocks = [normed_two, places.by_z(normed_two)]
    hn_blocks, back = [None] * ring, [None] * ring
    near(0)
    near(1)
    far(0)
    for j in range(ring):
        if j + 2 < ring:
            ring_blocks.append(places.by_z(ring_blocks[-1]))
            dy_first.append(places.by_z(dy_first[-1]))
            near(j + 2)
        if j + 1 < ring:
            far(j + 1)
        if j > 2:
            places.single = "z"
            back_near(j - 2)
            back_ring(j - 2)
        if j > 1:
            back_far(j - 1)
        run(j)
    last = ring - 1
    back_far(last)
    if last > 1:
        back_near(last - 1)
        back_ring(last - 1)
    places.after = None
    kept = lax.optimization_barrier((kept, results[last][2]))[0]
    expert_sums = grads_of(range(ring), ())
    places.after = expert_sums[1]
    back_near(last)
    back_far(0)
    near_last = back[last]
    places.after = back[0]
    back_ring(last)
    places.after = None
    back_near(0)
    mixture = lax.optimization_barrier((results[-1][1], near_last))[0]
    normed_grad = sum(part.astype(F32) for part in back)
    gate_grads = lax.all_to_all(
        results[-1][2].reshape(count, half), "dp", split_axis=0, concat_axis=0, tiled=True
    )
    gate_grads = jnp.sum(gate_grads.reshape(experts, splits, half), axis=1).T

    logits = jnp.where(named, dot(normed_two, w_router), NEGATIVE)
    gates = jax.nn.softmax(logits, axis=-1)
    logit_grad = gates * (gate_grads - jnp.sum(gates * gate_grads, axis=-1, keepdims=True))
    logit_grad = logit_grad.astype(BF16)
    grad_router = dot(logit_grad, normed_two, TN)
    normed_grad = normed_grad + dot(logit_grad, w_router, NT)
    grad_gain_two = jnp.sum(normed_grad * hidden * inverse_two, axis=0)
    hidden_grad = dy.astype(F32) + norm_back(hidden, inverse_two, gain_two, normed_grad)
    hidden_low = places.both_halves(hidden_grad.astype(BF16))
    mixture = lax.psum_scatter(mixture, "dp", scatter_dimension=0, tiled=True)
    mixture = mixture.astype(F32)
    grad_out = dot(mixed_heads, hidden_low, TN).astype(BF16)

    grad_heads_w, part = attend_back(
        hidden_low, w_query, w_key, w_value, w_out, *around, normed, queries, keys, values, sums
    )
    grad_heads_w = places.sum_all(grad_heads_w)
    begun = next(grad_heads_w)
    normed_grad_one = places.sum_halves(part)
    inverse_half = inverse_rms(inputs_half)
    grad_gain_one = jnp.sum(normed_grad_one * inputs_half * inverse_half, axis=0)
    grad_input = hidden_grad + norm_back(inputs_half, inverse_half, gain_one, normed_grad_one)
    grad_input = places.both_halves(grad_input.astype(BF16))

    small = jnp.concatenate([grad_router, grad_gain_one[None], grad_gain_two[None]], axis=0)
    small = (small + places.by_t(small)).astype(BF16)
    rows, columns = grad_out.shape
    spare = 256 * (-(-small.size // (256 * rows)))
    small = jnp.pad(small.reshape(-1), (0, rows * spare - small.size)).reshape(rows, spare)
    grad_out = places.sum_all(jnp.concatenate([grad_out, small], axis=1))
    next(grad_out)
    next(grad_heads_w)
    next(grad_out)
    next(grad_heads_w)
    next(grad_out)
    next(grad_heads_w)
    next(grad_out)
    grad_heads_w = next(grad_heads_w).astype(F32)
    grad_out = next(grad_out).astype(F32)
    small = grad_out[:, columns:].reshape(-1)[: (experts + 2) * model].reshape(-1, model)
    grad_out = grad_out[:, :columns]
    output = places.both_halves((hidden + mixture).astype(BF16))

    grad_gu = lax.psum_scatter(expert_sums[0], "tensor", scatter_dimension=0)
    grad_d = lax.psum_scatter(expert_sums[1], "tensor", scatter_dimension=0, tiled=True)
    width = w_gate.shape[2]
    query_width, key_width = w_query.shape[1], w_key.shape[1]
    return (
        output,
        grad_input,
        small[experts],
        grad_heads_w[:, :query_width],
        grad_heads_w[:, query_width : query_width + key_width],
        grad_heads_w[:, query_width + key_width :],
        grad_out,
        small[experts + 1],
        small[:experts].T,
        grad_gu[None, :, :width],
        grad_gu[None, :, width:],
        grad_d[None],
    )


def solution(mesh):
    in_specs = (
        P("dp", None),
        P("dp", None),
        P("dp", None),
        P(),
        P(None, "tensor"),
        P(None, "tensor"),
        P(None, "tensor"),
        P("tensor", None),
        P(),
        P(),
        P("dp", None, "tensor"),
        P("dp", None, "tensor"),
        P("dp", "tensor", None),
        P("dp", None),
    )
    out_specs = (
        P("dp", None),
        P("dp", None),
        P(),
        P(None, "tensor"),
        P(None, "tensor"),
        P(None, "tensor"),
        P("tensor", None),
        P(),
        P(),
        P("dp", None, "tensor"),
        P("dp", None, "tensor"),
        P("dp", "tensor", None),
    )
    return jax.shard_map(
        on_device, mesh=mesh, in_specs=in_specs, out_specs=out_specs, check_vma=False
    )
```
